256 devices in a mesh: mp: 4 (over y), seq: 16 (over x, z_lo, core), dp: 4 (over z_hi).
Axes of the slice: x: 4, y: 4, z: 8 (z_hi: 4, z_lo: 2; z = z_hi * 2 + z_lo), core: 2. Of those that a mesh axis runs over, the one named last changes fastest.
Arguments:
- gen_features: bfloat16 [4, 2048, 3072], P('dp', 'seq'), may hold values from -6 to 6
- gen_gain: bfloat16 [3072], replicated, may hold values from 0.5 to 1.5
- gen_weight: bfloat16 [3072, 64], replicated, may hold values from -0.109375 to 0.109375
- flow_noise: bfloat16 [4, 2048, 64], P('dp', 'seq'), may hold values from -133 to 133
- time_steps: int32 [4], P('dp'), may hold values from 0 to 999
- embed_weight: bfloat16 [2, 64, 3072], replicated, may hold values from -0.75 to 0.75
- norm_gain: bfloat16 [2, 3072], replicated, may hold values from 0.5 to 1.5
- qkv_weight: bfloat16 [2, 3072, 3, 2048], P(None, None, None, 'seq'), may hold values from -0.109375 to 0.109375
- qk_gain: bfloat16 [2, 2, 128], replicated, may hold values from 0.5 to 1.5
- out_weight: bfloat16 [2, 2048, 64], replicated, may hold values from -0.125 to 0.125
Outputs:
- dmd_grad: float32 [4, 2048, 64], P('dp', 'seq')
- gen_grad: float32 [3072, 64], P('seq')
The draws below stay inside these ranges and needn't reach their ends.
All inputs are finite; a program needn't handle non-finite values.
Results may differ from the reference program's by a relative error of at most 0.0065.
Values may be sent and summed in bfloat16 or wider, within the bound.
No kernel may reach another device: no remote copies, remote signals or barrier semaphores. Data moves between devices by JAX's collectives and lax.ppermute only.
A program may use at most 128 MiB of HBM per device.

```python
import math
import jax
import jax.numpy as jnp
from jax import lax

D = 3072
C = 64
HEADS = 16
HD = 128
STEPS = 1000
L = 2048
A = 2048
B = 4


def draw_flow_noise(key, part):
    key = jax.random.fold_in(key, 7)
    key_base, key_rows, key_cols = jax.random.split(key, 3)
    position = jnp.arange(L).astype(jnp.float32) / (L - 1)
    rising = 1.0 + 2.0 * position
    row_scale = jnp.exp(jax.random.uniform(key_rows, (B, L, 1)) * 1.2) * rising[None, :, None]
    col_scale = jnp.exp(jax.random.uniform(key_cols, (1, 1, C)) * 1.2)
    base = jnp.clip(jax.random.normal(key_base, (B, L, C)), -4.0, 4.0)
    return (base * row_scale * col_scale).astype(jnp.bfloat16)


def with_ends(array, rng, least, largest):
    extent = array.shape
    spot = [jax.random.randint(jax.random.fold_in(rng, axis), (), 0, extent[axis]) for axis in range(len(extent))]
    array = array.at[tuple(spot)].set(least)
    longest = extent.index(max(extent))
    spot[longest] = (spot[longest] + 1) % extent[longest]
    return array.at[tuple(spot)].set(largest)


def block_scale(stream_key, dims, cuts, least, top_value):
    loudness = 1.0
    for dim, shards_of in cuts:
        heights = jax.random.uniform(jax.random.fold_in(jax.random.fold_in(stream_key, 6), dim), (shards_of,), jnp.float32, least / len(cuts), top_value / len(cuts))
        loudness = loudness * jnp.repeat(jnp.exp(heights), dims[dim] // shards_of).reshape((-1,) + (1,) * (len(dims) - 1 - dim))
    return loudness


def normal_values(key, dims, scale, reach, pieces=(), dtype=jnp.bfloat16):
    drawn = jax.random.normal(key, dims, jnp.float32) * scale
    if len(pieces) > 0:
        drawn = block_scale(key, dims, pieces, -0.22, 0.18) * drawn
    return jnp.clip(drawn, min=-reach, max=reach).astype(dtype)


def setup_inputs(seed: int = 0) -> dict:
    keys = jax.random.split(jax.random.key(seed), 11)
    return {
        "gen_features": normal_values(keys[0], (B, L, D), 1.0, 6.0, ((0, 4), (1, 16))),
        "gen_gain": jnp.clip(1.0 + 0.1 * jax.random.normal(keys[1], (D,), jnp.float32), 0.5, 1.5).astype(jnp.bfloat16),
        "gen_weight": normal_values(keys[2], (D, C), D ** -0.5, 0.109375),
        "flow_noise": draw_flow_noise(jax.random.fold_in(keys[10], 71), 0),
        "time_steps": with_ends(jax.random.randint(keys[4], (B,), 0, STEPS), jax.random.fold_in(keys[4], 1), 0, STEPS - 1).astype(jnp.int32),
        "embed_weight": normal_values(keys[5], (2, C, D), C ** -0.5, 0.75),
        "norm_gain": jnp.clip(1.0 + 0.1 * jax.random.normal(keys[6], (2, D), jnp.float32), 0.5, 1.5).astype(jnp.bfloat16),
        "qkv_weight": normal_values(keys[7], (2, D, 3, A), D ** -0.5, 0.109375, ((3, 16),)),
        "qk_gain": jnp.clip(1.0 + 0.1 * jax.random.normal(keys[8], (2, 2, HD), jnp.float32), 0.5, 1.5).astype(jnp.bfloat16),
        "out_weight": normal_values(keys[9], (2, A, C), A ** -0.5, 0.125),
    }


def rms_scale(values, gain):
    mean_square = lax.optimization_barrier(jnp.mean(values * values, axis=-1, keepdims=True))
    return values * lax.rsqrt(mean_square + 1e-06) * gain.astype(jnp.float32)

def time_embedding(step_value, width):
    half_width = width // 2
    ranks = jnp.arange(half_width).astype(jnp.float32) / half_width
    frequency = jnp.exp(-math.log(10000.0) * ranks)
    phases = step_value * frequency
    return jnp.concatenate([jnp.cos(phases), jnp.sin(phases)])

def score_velocity(noisy_bf, step_value, embed_table, norm_scale, projection, gain_pair, out_table):
    hidden = jnp.dot(noisy_bf, embed_table, preferred_element_type=jnp.float32) + time_embedding(step_value, D)
    normed = rms_scale(hidden, norm_scale).astype(jnp.bfloat16)
    per_head = projection.reshape(D, 3, HEADS, HD).transpose(2, 0, 1, 3)

    def one_head(head_weight):
        projected = jnp.dot(normed, head_weight.reshape(D, 3 * HD), preferred_element_type=jnp.float32).reshape(L, 3, HD)
        query_rows = rms_scale(projected[:, 0], gain_pair[0]).astype(jnp.bfloat16)
        key_rows = rms_scale(projected[:, 1], gain_pair[1]).astype(jnp.bfloat16)
        value_rows = projected[:, 2].astype(jnp.bfloat16)
        scores = jnp.dot(query_rows, key_rows.T, preferred_element_type=jnp.float32) / math.sqrt(HD)
        weights = jnp.exp(scores)
        shares = (weights / lax.optimization_barrier(jnp.sum(weights, axis=1, keepdims=True))).astype(jnp.bfloat16)
        return jnp.dot(shares, value_rows, preferred_element_type=jnp.float32).astype(jnp.bfloat16)
    attended = lax.map(one_head, per_head)
    merged = attended.transpose(1, 0, 2).reshape(L, HEADS * HD)
    return jnp.dot(merged, out_table, preferred_element_type=jnp.float32)

def reference(gen_features, gen_gain, gen_weight, flow_noise, time_steps, embed_weight, norm_gain, qkv_weight, qk_gain, out_weight):

    def one_sample(inputs):
        features, noise_rows, step_index = inputs
        features_f = features.astype(jnp.float32)
        inv_rms = lax.rsqrt(lax.optimization_barrier(jnp.sum(features_f * features_f, axis=1)) / D + 1e-06)
        scaled = (features_f * gen_gain.astype(jnp.float32)).astype(jnp.bfloat16)
        clean = jnp.dot(scaled, gen_weight, preferred_element_type=jnp.float32) * inv_rms[:, None]
        step_value = step_index.astype(jnp.float32)
        level = (step_value + 1.0) / (STEPS + 1.0)
        noisy = (1.0 - level) * clean + level * noise_rows.astype(jnp.float32)
        noisy_bf = noisy.astype(jnp.bfloat16)
        predicted = []
        for model_index in range(2):
            velocity = score_velocity(noisy_bf, step_value, embed_weight[model_index], norm_gain[model_index], qkv_weight[model_index], qk_gain[model_index], out_weight[model_index])
            predicted.append(noisy - level * velocity)
        real_pred = predicted[0]
        fake_pred = predicted[1]
        weight = jnp.sum(jnp.abs(clean - real_pred)) / (L * C) + 1e-05
        gap = fake_pred - real_pred
        direction = (gap * inv_rms[:, None]).astype(jnp.bfloat16)
        partial_value = jnp.dot(scaled.T, direction, preferred_element_type=jnp.float32)
        return (gap / weight, partial_value / weight)
    dmd_grad, partials = lax.map(one_sample, (gen_features, flow_noise, time_steps))
    return (dmd_grad, lax.optimization_barrier(jnp.sum(partials, axis=0)))
```

```python
import math

import jax
import jax.numpy as jnp
from jax import lax
from jax.experimental import pallas as pl
from jax.experimental.pallas import tpu as pltpu
from jax.sharding import PartitionSpec as P

F32 = jnp.float32
BF16 = jnp.bfloat16
STEPS = 1000
NN = (((1,), (0,)), ((), ()))
NT = (((1,), (1,)), ((), ()))
TN = (((0,), (0,)), ((), ()))
VMEM = pl.BlockSpec(memory_space=pltpu.VMEM)
SMEM = pl.BlockSpec(memory_space=pltpu.SMEM)
VMEM_BYTES = 48 * 1024 * 1024


def dot(left, right, dims=NN):
    return lax.dot_general(left, right, dims, preferred_element_type=F32)


def split_two(values):
    high = values.astype(BF16)
    low = (values - high.astype(F32)).astype(BF16)
    return high, low


def level_of(steps_ref):
    return (steps_ref[0].astype(F32) + 1.0) * (1.0 / (STEPS + 1.0))


def time_embedding(step_value, width):
    half_width = width // 2
    ranks = jnp.arange(half_width).astype(F32) / half_width
    frequency = jnp.exp(-math.log(10000.0) * ranks)
    phases = step_value * frequency
    return jnp.concatenate([jnp.cos(phases), jnp.sin(phases)])


def scaled_and_rms(features, gain):
    features_f = features.astype(F32)
    mean_square = jnp.sum(features_f * features_f, axis=1, keepdims=True) / features.shape[1]
    return (features_f * gain).astype(BF16), lax.rsqrt(mean_square + 1e-06)


def latents_kernel(steps_ref, features_ref, gain_ref, weight_ref, noise_ref, send_ref, clean_ref, noisy_ref):
    level = level_of(steps_ref)
    slot = lax.axis_index("mp")
    tokens = features_ref.shape[0]
    part = tokens // 4
    rows = [features_ref[pl.ds(pl.multiple_of(((slot + i) % 4) * part, part), part), :] for i in range(4)]
    scaled, inv_rms = scaled_and_rms(jnp.concatenate(rows, axis=0), gain_ref[...].astype(F32))
    inv_row = jnp.broadcast_to(inv_rms, (tokens, tokens)).T[0:1]
    clean = dot(weight_ref[...], scaled, NT) * inv_row
    noise = pltpu.roll(noise_ref[...].astype(F32), (tokens - slot * part) % tokens, 1)
    noisy = (1.0 - level) * clean + level * noise
    rounded = noisy.astype(BF16)
    for target in range(send_ref.shape[0]):
        send_ref[target] = rounded
    clean_ref[...] = clean
    noisy_ref[...] = noisy


def own_kernel(features_ref, gain_ref, clean_ref, noisy_ref, scaled_ref, own_ref, inv_ref):
    tokens = features_ref.shape[0]
    part = tokens // 4
    slot = lax.axis_index("mp")
    rows = features_ref[pl.ds(pl.multiple_of(slot * part, part), part), :]
    scaled, inv_rms = scaled_and_rms(rows, gain_ref[...].astype(F32))
    scaled_ref[...] = scaled
    inv_ref[...] = jnp.broadcast_to(inv_rms, inv_ref.shape)
    both = jnp.concatenate([clean_ref[...], noisy_ref[...]], axis=0).T
    own_ref[...] = both[0:part]


def fold_kernel(temb_ref, embed_ref, gain_ref, qkv_ref, qk_ref, out_ref, fold_ref, scale_ref, square_ref, acc, gram):
    step = pl.program_id(0)
    chunk = embed_ref.shape[2]

    @pl.when(step == 0)
    def _():
        acc[...] = jnp.zeros_like(acc)
        gram[...] = jnp.zeros_like(gram)
        square_ref[...] = jnp.zeros_like(square_ref)

    temb = temb_ref[...]
    squares = jnp.sum(temb * temb, axis=1, keepdims=True)
    square_ref[...] += jnp.broadcast_to(squares, square_ref.shape)
    spot = lax.broadcasted_iota(jnp.int32, (16, chunk), 0)
    temb_one = temb.astype(BF16).astype(F32)
    temb_two = (temb - temb_one).astype(BF16).astype(F32)
    temb_three = temb - temb_one - temb_two
    temb_rows = jnp.where(spot == 0, temb_one, jnp.where(spot == 1, temb_two, jnp.where(spot == 2, temb_three, 0.0))).astype(BF16)
    for m in range(2):
        gain = gain_ref[m : m + 1, :].astype(F32)
        table = embed_ref[m]
        high, low = split_two(table.astype(F32) * gain)
        biased = temb * gain
        bias_high = biased.astype(BF16).astype(F32)
        bias_rows = jnp.where(spot == 0, bias_high, jnp.where(spot == 1, biased - bias_high, 0.0)).astype(BF16)
        rows = jnp.concatenate([high, low, bias_rows], axis=0)
        for i in range(3):
            acc[m, i] += dot(rows, qkv_ref[m, i])
        pads = jnp.zeros((48, chunk), BF16)
        gram[m] += dot(table, jnp.concatenate([table, temb_rows, pads], axis=0), NT)

    @pl.when(step == pl.num_programs(0) - 1)
    def _():
        head = lax.axis_index("seq")
        lane = lax.broadcasted_iota(jnp.int32, (64, 128), 1)
        row = lax.broadcasted_iota(jnp.int32, (64, 128), 0)

        def stacked(m, i):
            whole = acc[m, i]
            table = whole[0:64] + whole[64:128]
            bias = whole[128:129] + whole[129:130]
            return jnp.concatenate([table, jnp.where(row == 0, bias, 0.0)], axis=0)

        for m in range(2):
            value_high, value_low = split_two(stacked(m, 2))
            out_rows = out_ref[m, :, pl.ds(pl.multiple_of(head * 128, 128), 128)]
            mixed = dot(out_rows, value_high, NT) + dot(out_rows, value_low, NT)
            inner = gram[m]
            linear = inner[:, 64:65] + inner[:, 65:66] + inner[:, 66:67]
            inner = jnp.where(lane < 64, inner, jnp.where(lane == 64, 2.0 * linear, 0.0))
            whole = jnp.concatenate([stacked(m, 1).T, mixed, inner, stacked(m, 0).T], axis=0)
            high, low = split_two(whole)
            fold_ref[m] = jnp.concatenate([high, low], axis=1)
            gains = qk_ref[m, 0:1, :].astype(F32) * qk_ref[m, 1:2, :].astype(F32)
            gains = gains * (math.log2(math.e) / math.sqrt(128.0))
            scale_ref[m] = jnp.broadcast_to(gains, (128, 128)).T


def attention_kernel(latent_ref, fold_ref, scale_ref, square_ref, send_ref, latents, queries):
    blocks = latent_ref.shape[0]
    keys = blocks * 128
    count = blocks * 32
    latents[...] = jnp.ones_like(latents)
    queries[...] = jnp.ones_like(queries)
    for s in range(blocks):
        block = latent_ref[s]
        latents[0:64, s * 128 : (s + 1) * 128] = block
        latents[128:192, s * 128 : (s + 1) * 128] = block
    for g in range(blocks // 4):
        pieces = jnp.concatenate([latent_ref[4 * g + i][:, 0:32] for i in range(4)], axis=1)
        queries[0:64, g * 128 : (g + 1) * 128] = pieces
        queries[128:192, g * 128 : (g + 1) * 128] = pieces
    squares = square_ref[0:1, 0:1]

    def hidden_square(inner, rows):
        return (jnp.sum(inner * rows.astype(F32), axis=0, keepdims=True) + squares) / 3072.0 + 1e-06

    mixed = []
    for m in range(2):
        projected = dot(fold_ref[m, 0:256], latents[...])
        hidden = hidden_square(projected[192:256], latents[0:64])
        key = projected[0:128]
        key_scale = lax.rsqrt(jnp.mean(key * key, axis=0, keepdims=True) + 1e-06 * hidden)
        key = (key * key_scale).astype(BF16)
        value = (projected[128:192] * lax.rsqrt(hidden)).astype(BF16)
        value = jnp.concatenate([value, jnp.ones((16, keys), BF16)], axis=0)
        projected = dot(fold_ref[m, 192:384], queries[...])
        hidden = hidden_square(projected[0:64], queries[0:64])
        query = projected[64:192]
        query_scale = lax.rsqrt(jnp.mean(query * query, axis=0, keepdims=True) + 1e-06 * hidden)
        query = query * query_scale * jnp.concatenate([scale_ref[m]] * (count // 128), axis=1)
        query = query.astype(BF16).T
        total = jnp.zeros((80, count), F32)
        for c in range(keys // 512):
            span = slice(c * 512, (c + 1) * 512)
            shares = jnp.exp2(dot(query, key[:, span])).astype(BF16)
            total += dot(value[:, span], shares, NT)
        mixed.append(total[0:64] / total[64:65])
    whole = jnp.concatenate(mixed, axis=0).T.astype(BF16)
    send_ref[...] = whole.reshape(send_ref.shape)


def spread_rows(total, width):
    spot = lax.broadcasted_iota(jnp.int32, (16, width), 0)
    high = total.astype(BF16).astype(F32)
    return jnp.where(spot == 0, high, jnp.where(spot == 1, total - high, 0.0)).astype(BF16)


def gap_kernel(steps_ref, velocity_ref, scaled_ref, own_ref, inv_ref, send_ref, gap_ref):
    level = level_of(steps_ref)
    velocity = jnp.sum(velocity_ref[...].astype(F32), axis=0)
    own = own_ref[...]
    teacher = velocity[:, 0:64]
    gap = level * (teacher - velocity[:, 64:128])
    distance = jnp.abs(own[:, 0:64] - (own[:, 64:128] - level * teacher))
    spread = jnp.sum(jnp.sum(distance, axis=1, keepdims=True), axis=0, keepdims=True)
    direction = (gap * inv_ref[:, 0:64]).astype(BF16)
    high = gap.astype(BF16)
    gap_ref[...] = jnp.concatenate([high, (gap - high.astype(F32)).astype(BF16)], axis=1)
    grad = dot(direction, scaled_ref[...], TN)
    tail = spread_rows(jnp.broadcast_to(spread, (1, 128)), 128)
    left = lax.broadcasted_iota(jnp.int32, (32, 128), 1) < 64
    for j in range(send_ref.shape[0] // 2):
        first = grad[:, j * 384 : j * 384 + 128]
        middle = grad[:, j * 384 + 128 : j * 384 + 256]
        last = grad[:, j * 384 + 256 : j * 384 + 384]
        turned = pltpu.roll(middle, 64, 1)
        even = jnp.where(left, middle[0:32], turned[32:64])
        odd = jnp.where(left, turned[0:32], middle[32:64])
        send_ref[2 * j] = jnp.concatenate([first.astype(BF16), even.astype(BF16), tail], axis=0)
        send_ref[2 * j + 1] = jnp.concatenate([last.astype(BF16), odd.astype(BF16), tail], axis=0)


def total_kernel(grad_ref, gap_ref, send_ref):
    total = jnp.sum(grad_ref[...].astype(F32), axis=0)
    tail = spread_rows(total[96:97] + total[97:98], 128)
    whole = jnp.concatenate([total[0:96].astype(BF16), tail, gap_ref[...]], axis=0)
    for target in range(send_ref.shape[0]):
        send_ref[target] = whole


def result_kernel(all_ref, gap_ref, grad_ref):
    weights = []
    total = jnp.zeros((96, 128), F32)
    for d in range(4):
        parts = jnp.sum(jnp.stack([all_ref[4 * m + d, 0:112].astype(F32) for m in range(4)]), axis=0)
        inverse = 1.0 / ((parts[96:97] + parts[97:98]) / 131072.0 + 1e-05)
        total += parts[0:96] * inverse
        weights.append(inverse)
    sample = lax.axis_index("dp")
    inverse = weights[0]
    for d in range(1, 4):
        inverse = jnp.where(sample == d, weights[d], inverse)
    gaps = []
    for m in range(4):
        pair = all_ref[4 * m + sample, 112:144].astype(F32)
        gaps.append(pair + pltpu.roll(pair, 64, 1))
    gap_ref[...] = (jnp.concatenate(gaps, axis=0) * inverse).T[0:64]
    whole = total[0:64]
    low = total[64:96]
    half = jnp.concatenate([low, pltpu.roll(low, 64, 1)], axis=0)
    odd = lax.axis_index("seq") % 2 == 1

    @pl.when(odd)
    def _():
        grad_ref[:, 0:64] = half[:, 0:64]
        grad_ref[:, 64:192] = whole

    @pl.when(jnp.logical_not(odd))
    def _():
        grad_ref[:, 0:128] = whole
        grad_ref[:, 128:192] = half[:, 0:64]


def call(kernel, outs, in_specs, name, flops=0, moved=0, **more):
    return pl.pallas_call(
        kernel,
        out_shape=outs,
        in_specs=in_specs,
        out_specs=more.pop("out_specs", jax.tree.map(lambda _: VMEM, outs)),
        compiler_params=pltpu.CompilerParams(vmem_limit_bytes=VMEM_BYTES),
        cost_estimate=pl.CostEstimate(flops=flops, bytes_accessed=moved, transcendentals=0),
        name=name,
        **more,
    )


def per_device(
    gen_features,
    gen_gain,
    gen_weight,
    flow_noise,
    time_steps,
    embed_weight,
    norm_gain,
    qkv_weight,
    qk_gain,
    out_weight,
):
    shape = jax.ShapeDtypeStruct
    seq_count = lax.axis_size("seq")
    group = lax.axis_size("mp") * lax.axis_size("dp")
    features = gen_features[0]
    tokens, width = features.shape
    part = tokens // 4
    gain_row = gen_gain[None]
    send, clean, noisy = call(
        latents_kernel,
        (shape((seq_count, 64, tokens), BF16), shape((64, tokens), F32), shape((64, tokens), F32)),
        [SMEM, VMEM, VMEM, VMEM, VMEM],
        "latents",
        flops=2 * tokens * width * 64,
        moved=2 * tokens * width,
    )(time_steps, features, gain_row, gen_weight.T, flow_noise[0].T)
    every_latent = lax.all_to_all(send, "seq", 0, 0)

    scaled, own, inv = call(
        own_kernel,
        (shape((part, width), BF16), shape((part, 128), F32), shape((part, 128), F32)),
        [VMEM] * 4,
        "own",
        flops=part * width * 4,
        moved=2 * tokens * width,
    )(features, gain_row, clean, noisy)
    temb = time_embedding(time_steps[0].astype(F32), width)[None]
    chunk = 512
    fold, scale, square = call(
        fold_kernel,
        (shape((2, 384, 256), BF16), shape((2, 128, 128), F32), shape((8, 128), F32)),
        [
            pl.BlockSpec((1, chunk), lambda k: (0, k)),
            pl.BlockSpec((2, 64, chunk), lambda k: (0, 0, k)),
            pl.BlockSpec((2, chunk), lambda k: (0, k)),
            pl.BlockSpec((2, 3, chunk, 128), lambda k: (0, 0, k, 0)),
            pl.BlockSpec((2, 2, 128), lambda k: (0, 0, 0)),
            pl.BlockSpec((2, 64, 2048), lambda k: (0, 0, 0)),
        ],
        "fold",
        flops=2 * 2 * width * 384 * 256,
        moved=2 * 2 * width * 384,
        out_specs=(
            pl.BlockSpec((2, 384, 256), lambda k: (0, 0, 0)),
            pl.BlockSpec((2, 128, 128), lambda k: (0, 0, 0)),
            pl.BlockSpec((8, 128), lambda k: (0, 0)),
        ),
        grid=(width // chunk,),
        scratch_shapes=[pltpu.VMEM((2, 3, 144, 128), F32), pltpu.VMEM((2, 64, 128), F32)],
    )(
        temb,
        embed_weight,
        norm_gain,
        qkv_weight.transpose(0, 2, 1, 3),
        qk_gain,
        out_weight.transpose(0, 2, 1),
    )
    keys = seq_count * tokens
    send = call(
        attention_kernel,
        shape((seq_count, part, 128), BF16),
        [VMEM] * 4,
        "attention",
        flops=2 * 2 * keys * (keys // 4) * 256,
        moved=2 * keys * 64,
        scratch_shapes=[pltpu.VMEM((256, keys), BF16), pltpu.VMEM((256, keys // 4), BF16)],
    )(every_latent, fold, scale, square)
    velocities = lax.all_to_all(send, "seq", 0, 0)
    send, gap = call(
        gap_kernel,
        (shape((seq_count, 112, 128), BF16), shape((part, 128), BF16)),
        [SMEM] + [VMEM] * 4,
        "gap",
        flops=2 * part * width * 64,
        moved=2 * part * width,
    )(time_steps, velocities, scaled, own, inv)
    partials = lax.all_to_all(send, "seq", 0, 0)
    send = call(
        total_kernel,
        shape((group, 144, 128), BF16),
        [VMEM] * 2,
        "total",
        flops=seq_count * 112 * 128,
        moved=2 * seq_count * 112 * 128,
    )(partials, gap)
    every_total = lax.all_to_all(send, ("mp", "dp"), 0, 0)
    dmd, grad = call(
        result_kernel,
        (shape((64, tokens), F32), shape((64, width // seq_count), F32)),
        [VMEM],
        "result",
        flops=group * 112 * 128,
        moved=2 * group * 144 * 128,
    )(every_total)
    return dmd.T[None], grad.T


def solution(mesh):
    placed = (
        P("dp", "seq", None),
        P(),
        P(),
        P("dp", "seq", None),
        P("dp"),
        P(),
        P(),
        P(None, None, None, "seq"),
        P(),
        P(),
    )
    return jax.shard_map(
        per_device,
        mesh=mesh,
        in_specs=placed,
        out_specs=(P("dp", "seq", None), P("seq", None)),
        check_vma=False,
    )
```

```python
import math

import jax
import jax.numpy as jnp
from jax import lax
from jax.experimental import pallas as pl
from jax.experimental.pallas import tpu as pltpu
from jax.sharding import PartitionSpec as P

F32 = jnp.float32
BF16 = jnp.bfloat16
STEPS = 1000
NN = (((1,), (0,)), ((), ()))
NT = (((1,), (1,)), ((), ()))
TN = (((0,), (0,)), ((), ()))
VMEM = pl.BlockSpec(memory_space=pltpu.VMEM)
SMEM = pl.BlockSpec(memory_space=pltpu.SMEM)
HBM = pl.BlockSpec(memory_space=pltpu.HBM)
VMEM_BYTES = 48 * 1024 * 1024


def dot(left, right, dims=NN):
    return lax.dot_general(left, right, dims, preferred_element_type=F32)


def split_two(values):
    high = values.astype(BF16)
    low = (values - high.astype(F32)).astype(BF16)
    return high, low


def level_of(steps_ref):
    return (steps_ref[0].astype(F32) + 1.0) * (1.0 / (STEPS + 1.0))


def time_embedding(step_value, width):
    half_width = width // 2
    ranks = jnp.arange(half_width).astype(F32) / half_width
    frequency = jnp.exp(-math.log(10000.0) * ranks)
    phases = step_value * frequency
    return jnp.concatenate([jnp.cos(phases), jnp.sin(phases)])


def scaled_and_rms(features, gain):
    features_f = features.astype(F32)
    mean_square = jnp.sum(features_f * features_f, axis=1, keepdims=True) / features.shape[1]
    return (features_f * gain).astype(BF16), lax.rsqrt(mean_square + 1e-06)


def latents_kernel(steps_ref, features_hbm, gain_hbm, weight_hbm, noise_hbm, send_ref, features, gain, weight, noise, sems):
    slot = lax.axis_index("mp")
    tokens, width = features.shape
    part = tokens // 4
    copies = [
        pltpu.make_async_copy(gain_hbm, gain, sems.at[4]),
        pltpu.make_async_copy(weight_hbm, weight, sems.at[5]),
        pltpu.make_async_copy(noise_hbm, noise, sems.at[6]),
    ]
    quarters = []
    for i in range(4):
        start = pl.multiple_of(((slot + i) % 4) * part, part)
        rows = features.at[pl.ds(i * part, part), :]
        quarters.append(pltpu.make_async_copy(features_hbm.at[pl.ds(start, part), :], rows, sems.at[i]))
    for copy in copies[:1] + quarters + copies[1:]:
        copy.start()
    level = level_of(steps_ref)
    copies[0].wait()
    gain_row = gain[...].astype(F32).reshape(1, width)
    scaled, inverse = [], []
    for i in range(4):
        quarters[i].wait()
        one, inv_rms = scaled_and_rms(features[i * part : (i + 1) * part, :], gain_row)
        scaled.append(one)
        inverse.append(inv_rms)
    inv_row = jnp.broadcast_to(jnp.concatenate(inverse, axis=0), (tokens, tokens)).T[0:1]
    copies[1].wait()
    clean = dot(weight[...], jnp.concatenate(scaled, axis=0), NT) * inv_row
    copies[2].wait()
    noise_here = pltpu.roll(noise[...].astype(F32), (tokens - slot * part) % tokens, 1)
    rounded = ((1.0 - level) * clean + level * noise_here).astype(BF16)
    for target in range(send_ref.shape[0]):
        send_ref[target] = rounded


def own_kernel(steps_ref, features_hbm, gain_hbm, weight_hbm, noise_hbm, picked_ref, own_ref, inv_ref, features, gain, weight, noise, turned, sems):
    slot = lax.axis_index("mp")
    width = features.shape[1]
    pairs = ((gain_hbm, gain), (features_hbm, features), (weight_hbm, weight), (noise_hbm, noise))
    copies = [pltpu.make_async_copy(source, target, sems.at[i]) for i, (source, target) in enumerate(pairs)]
    for copy in copies:
        copy.start()
    for copy in copies:
        copy.wait()
    level = level_of(steps_ref)
    scaled, inv_rms = scaled_and_rms(features[...], gain[...].astype(F32).reshape(1, width))
    inv_ref[...] = jnp.broadcast_to(inv_rms, inv_ref.shape)
    clean = dot(scaled, weight[...], NT) * inv_rms
    noise_rows = noise[...].astype(F32).T
    own_ref[...] = jnp.concatenate([clean, (1.0 - level) * clean + level * noise_rows], axis=1)
    turned[...] = scaled.T
    for s in range(16):
        start = pl.multiple_of(s * 192 + slot * 48, 16)
        picked_ref[s * 48 : (s + 1) * 48, :] = turned[pl.ds(start, 48), :]


def fold_kernel(temb_ref, embed_hbm, gain_hbm, qkv_hbm, qk_hbm, out_hbm, fold_ref, scale_ref, square_ref, embed, gain, qkv, qk, out, sems):
    head = lax.axis_index("seq")
    width = embed.shape[2]
    parts = 3
    chunk = width // parts
    columns = pl.ds(pl.multiple_of(head * 128, 128), 128)
    pairs = ((embed_hbm, embed), (gain_hbm, gain), (qk_hbm, qk), (out_hbm.at[:, :, columns], out))
    copies = [pltpu.make_async_copy(source, target, sems.at[i]) for i, (source, target) in enumerate(pairs)]
    pieces = []
    for k in range(parts):
        span = pl.ds(k * chunk, chunk)
        pieces.append(pltpu.make_async_copy(qkv_hbm.at[:, :, span, :], qkv.at[:, :, span, :], sems.at[4 + k]))
    for copy in copies + pieces:
        copy.start()
    temb = temb_ref[...]
    squares = jnp.sum(temb * temb, axis=1, keepdims=True)
    square_ref[...] = jnp.broadcast_to(squares, square_ref.shape)
    spot = lax.broadcasted_iota(jnp.int32, (16, width), 0)
    temb_one = temb.astype(BF16).astype(F32)
    temb_two = (temb - temb_one).astype(BF16).astype(F32)
    temb_three = temb - temb_one - temb_two
    temb_rows = jnp.where(spot == 0, temb_one, jnp.where(spot == 1, temb_two, jnp.where(spot == 2, temb_three, 0.0))).astype(BF16)
    for copy in copies:
        copy.wait()
    rows, gram = [], []
    pads = jnp.zeros((48, width), BF16)
    for m in range(2):
        gain_row = gain[m : m + 1, :].astype(F32)
        table = embed[m]
        high, low = split_two(table.astype(F32) * gain_row)
        biased = temb * gain_row
        bias_high = biased.astype(BF16).astype(F32)
        bias_rows = jnp.where(spot == 0, bias_high, jnp.where(spot == 1, biased - bias_high, 0.0)).astype(BF16)
        rows.append(jnp.concatenate([high, low, bias_rows], axis=0))
        gram.append(dot(table, jnp.concatenate([table, temb_rows, pads], axis=0), NT))
    acc = [None, None]
    for k in range(parts):
        pieces[k].wait()
        span = slice(k * chunk, (k + 1) * chunk)
        for m in range(2):
            table = jnp.concatenate([qkv[m, i, span, :] for i in range(3)], axis=1)
            one = dot(rows[m][:, span], table)
            acc[m] = one if acc[m] is None else acc[m] + one
    lane = lax.broadcasted_iota(jnp.int32, (64, 128), 1)
    row = lax.broadcasted_iota(jnp.int32, (64, 128), 0)

    def stacked(m, i):
        whole = acc[m][:, i * 128 : (i + 1) * 128]
        table = whole[0:64] + whole[64:128]
        bias = whole[128:129] + whole[129:130]
        return jnp.concatenate([table, jnp.where(row == 0, bias, 0.0)], axis=0)

    for m in range(2):
        value_high, value_low = split_two(stacked(m, 2))
        mixed = dot(out[m], value_high, NT) + dot(out[m], value_low, NT)
        inner = gram[m]
        linear = inner[:, 64:65] + inner[:, 65:66] + inner[:, 66:67]
        inner = jnp.where(lane < 64, inner, jnp.where(lane == 64, 2.0 * linear, 0.0))
        whole = jnp.concatenate([stacked(m, 1).T, mixed, inner, stacked(m, 0).T], axis=0)
        high, low = split_two(whole)
        fold_ref[m] = jnp.concatenate([high, low], axis=1)
        gains = qk[m, 0:1, :].astype(F32) * qk[m, 1:2, :].astype(F32)
        gains = gains * (math.log2(math.e) / math.sqrt(128.0))
        scale_ref[m] = jnp.broadcast_to(gains, (128, 128)).T


def attention_kernel(latent_ref, fold_ref, scale_ref, square_ref, send_ref, latents, queries):
    blocks = latent_ref.shape[0]
    keys = blocks * 128
    count = blocks * 32
    latents[...] = jnp.ones_like(latents)
    queries[...] = jnp.ones_like(queries)
    for s in range(blocks):
        block = latent_ref[s]
        latents[0:64, s * 128 : (s + 1) * 128] = block
        latents[128:192, s * 128 : (s + 1) * 128] = block
    for g in range(blocks // 4):
        pieces = jnp.concatenate([latent_ref[4 * g + i][:, 0:32] for i in range(4)], axis=1)
        queries[0:64, g * 128 : (g + 1) * 128] = pieces
        queries[128:192, g * 128 : (g + 1) * 128] = pieces
    squares = square_ref[0:1, 0:1]

    def hidden_square(inner, rows):
        return (jnp.sum(inner * rows.astype(F32), axis=0, keepdims=True) + squares) / 3072.0 + 1e-06

    mixed = []
    for m in range(2):
        projected = dot(fold_ref[m, 0:256], latents[...])
        hidden = hidden_square(projected[192:256], latents[0:64])
        key = projected[0:128]
        key_scale = lax.rsqrt(jnp.mean(key * key, axis=0, keepdims=True) + 1e-06 * hidden)
        key = (key * key_scale).astype(BF16)
        value = (projected[128:192] * lax.rsqrt(hidden)).astype(BF16)
        value = jnp.concatenate([value, jnp.ones((16, keys), BF16)], axis=0)
        projected = dot(fold_ref[m, 192:384], queries[...])
        hidden = hidden_square(projected[0:64], queries[0:64])
        query = projected[64:192]
        query_scale = lax.rsqrt(jnp.mean(query * query, axis=0, keepdims=True) + 1e-06 * hidden)
        query = query * query_scale * jnp.concatenate([scale_ref[m]] * (count // 128), axis=1)
        query = query.astype(BF16).T
        total = jnp.zeros((80, count), F32)
        for c in range(keys // 512):
            span = slice(c * 512, (c + 1) * 512)
            shares = jnp.exp2(dot(query, key[:, span])).astype(BF16)
            total += dot(value[:, span], shares, NT)
        mixed.append(total[0:64] / total[64:65])
    whole = jnp.concatenate(mixed, axis=0).T.astype(BF16)
    for target in range(send_ref.shape[0]):
        s = target % blocks
        send_ref[target] = whole[s * 32 : (s + 1) * 32]


def gap_kernel(steps_ref, velocity_ref, picked_ref, own_ref, inv_ref, send_ref, gap_ref):
    level = level_of(steps_ref)
    blocks = send_ref.shape[0]
    velocity = [jnp.sum(velocity_ref[q * blocks : (q + 1) * blocks].astype(F32), axis=0) for q in range(4)]
    velocity = jnp.concatenate(velocity, axis=0)
    own = own_ref[...]
    teacher = velocity[:, 0:64]
    gap = level * (teacher - velocity[:, 64:128])
    gap_ref[...] = jnp.concatenate([gap, gap], axis=1)
    distance = jnp.abs(own[:, 0:64] - (own[:, 64:128] - level * teacher))
    spread = jnp.sum(jnp.sum(distance, axis=1, keepdims=True), axis=0, keepdims=True)
    direction = (gap * inv_ref[:, 0:64]).astype(BF16)
    grad = dot(picked_ref[...], jnp.concatenate([direction, direction], axis=1))
    spread = jnp.broadcast_to(spread, (8, 128))
    spot = lax.broadcasted_iota(jnp.int32, (8, 128), 0)
    high = spread.astype(BF16).astype(F32)
    tail = jnp.where(spot == 0, high, jnp.where(spot == 1, spread - high, 0.0))
    left = lax.broadcasted_iota(jnp.int32, (24, 128), 1) < 64
    for s in range(blocks):
        packed = jnp.where(left, grad[s * 48 : s * 48 + 24], grad[s * 48 + 24 : s * 48 + 48])
        send_ref[s] = jnp.concatenate([packed, tail], axis=0).astype(BF16)


def weight_inverse(total):
    return 1.0 / ((total[24:25] + total[25:26]) / 131072.0 + 1e-05)


def total_kernel(grad_ref, send_ref):
    total = jnp.sum(grad_ref[...].astype(F32), axis=0)
    whole = (total[0:24] * weight_inverse(total)).astype(BF16)
    for target in range(send_ref.shape[0]):
        send_ref[target] = whole


def dmd_kernel(grad_ref, gap_ref, dmd_ref):
    total = jnp.sum(grad_ref[...].astype(F32), axis=0)
    dmd_ref[...] = (gap_ref[...] * weight_inverse(total)).T[0:64]


def result_kernel(all_ref, grad_ref):
    rows = []
    for m in range(4):
        total = jnp.sum(all_ref[4 * m : 4 * m + 4].astype(F32), axis=0)
        rows += [total, pltpu.roll(total, 64, 1)]
    rows.append(jnp.zeros((64, 128), F32))
    grad_ref[...] = jnp.concatenate(rows, axis=0).T[0:64, 0:192]


def call(kernel, outs, in_specs, name, flops=0, moved=0, **more):
    return pl.pallas_call(
        kernel,
        out_shape=outs,
        in_specs=in_specs,
        out_specs=more.pop("out_specs", jax.tree.map(lambda _: VMEM, outs)),
        compiler_params=pltpu.CompilerParams(vmem_limit_bytes=VMEM_BYTES),
        cost_estimate=pl.CostEstimate(flops=flops, bytes_accessed=moved, transcendentals=0),
        name=name,
        **more,
    )


def per_device(
    gen_features,
    gen_gain,
    gen_weight,
    flow_noise,
    time_steps,
    embed_weight,
    norm_gain,
    qkv_weight,
    qk_gain,
    out_weight,
):
    shape = jax.ShapeDtypeStruct
    seq_count = lax.axis_size("seq")
    group = lax.axis_size("mp") * lax.axis_size("dp")
    features = gen_features[0]
    tokens, width = features.shape
    part = tokens // 4
    local = (time_steps, features, gen_gain, gen_weight.T, flow_noise[0].T)
    buffers = [
        pltpu.VMEM((tokens, width), BF16),
        pltpu.VMEM((width,), BF16),
        pltpu.VMEM((64, width), BF16),
        pltpu.VMEM((64, tokens), BF16),
    ]
    send = call(
        latents_kernel,
        shape((seq_count, 64, tokens), BF16),
        [SMEM] + [HBM] * 4,
        "latents",
        flops=2 * tokens * width * 64,
        moved=2 * tokens * width,
        scratch_shapes=buffers + [pltpu.SemaphoreType.DMA((7,))],
    )(*local)
    every_latent = lax.all_to_all(send, "seq", 0, 0)

    temb = time_embedding(time_steps[0].astype(F32), width)[None]
    fold, scale, square = call(
        fold_kernel,
        (shape((2, 384, 256), BF16), shape((2, 128, 128), F32), shape((8, 128), F32)),
        [VMEM] + [HBM] * 5,
        "fold",
        flops=2 * 2 * width * 384 * 256,
        moved=2 * 2 * width * 384,
        scratch_shapes=[
            pltpu.VMEM((2, 64, width), BF16),
            pltpu.VMEM((2, width), BF16),
            pltpu.VMEM((2, 3, width, 128), BF16),
            pltpu.VMEM((2, 2, 128), BF16),
            pltpu.VMEM((2, 64, 128), BF16),
            pltpu.SemaphoreType.DMA((7,)),
        ],
    )(
        temb,
        embed_weight,
        norm_gain,
        qkv_weight.transpose(0, 2, 1, 3),
        qk_gain,
        out_weight.transpose(0, 2, 1),
    )
    keys = seq_count * tokens
    send = call(
        attention_kernel,
        shape((4 * seq_count, part, 128), BF16),
        [VMEM] * 4,
        "attention",
        flops=2 * 2 * keys * (keys // 4) * 256,
        moved=2 * keys * 64,
        scratch_shapes=[pltpu.VMEM((256, keys), BF16), pltpu.VMEM((256, keys // 4), BF16)],
    )(every_latent, fold, scale, square)
    velocities = lax.all_to_all(send, ("mp", "seq"), 0, 0)
    picked, own, inv = call(
        own_kernel,
        (shape((width // 4, tokens), BF16), shape((tokens, 128), F32), shape((tokens, 128), F32)),
        [SMEM] + [HBM] * 4,
        "own",
        flops=2 * tokens * width * 64,
        moved=2 * tokens * width,
        scratch_shapes=buffers + [pltpu.VMEM((width, tokens), BF16), pltpu.SemaphoreType.DMA((4,))],
    )(*local)
    send, gap = call(
        gap_kernel,
        (shape((seq_count, 32, 128), BF16), shape((tokens, 128), F32)),
        [SMEM] + [VMEM] * 4,
        "gap",
        flops=2 * tokens * width * 16,
        moved=2 * 64 * 32 * 128,
    )(time_steps, velocities, picked, own, inv)
    partials = lax.all_to_all(send, "seq", 0, 0)
    send = call(
        total_kernel,
        shape((group, 24, 128), BF16),
        [VMEM],
        "total",
        flops=seq_count * 32 * 128,
        moved=2 * seq_count * 32 * 128,
    )(partials)
    every_total = lax.all_to_all(send, ("mp", "dp"), 0, 0)
    dmd = call(
        dmd_kernel,
        shape((64, tokens), F32),
        [VMEM] * 2,
        "dmd",
        flops=seq_count * 32 * 128,
        moved=2 * seq_count * 32 * 128,
    )(partials, gap)
    grad = call(
        result_kernel,
        shape((64, width // seq_count), F32),
        [VMEM],
        "result",
        flops=group * 24 * 128,
        moved=2 * group * 24 * 128,
    )(every_total)
    return dmd.T[None], grad.T


def solution(mesh):
    placed = (
        P("dp", "seq", None),
        P(),
        P(),
        P("dp", "seq", None),
        P("dp"),
        P(),
        P(),
        P(None, None, None, "seq"),
        P(),
        P(),
    )
    return jax.shard_map(
        per_device,
        mesh=mesh,
        in_specs=placed,
        out_specs=(P("dp", "seq", None), P("seq", None)),
        check_vma=False,
    )
```

```python
import math

import jax
import jax.numpy as jnp
from jax import lax
from jax.experimental import pallas as pl
from jax.experimental.pallas import tpu as pltpu
from jax.sharding import PartitionSpec as P

F32 = jnp.float32
BF16 = jnp.bfloat16
STEPS = 1000
NN = (((1,), (0,)), ((), ()))
NT = (((1,), (1,)), ((), ()))
TN = (((0,), (0,)), ((), ()))
VMEM = pl.BlockSpec(memory_space=pltpu.VMEM)
SMEM = pl.BlockSpec(memory_space=pltpu.SMEM)
HBM = pl.BlockSpec(memory_space=pltpu.HBM)
MEBI = 1024 * 1024


def dot(left, right, dims=NN):
    return lax.dot_general(left, right, dims, preferred_element_type=F32)


def split_two(values):
    high = values.astype(BF16)
    low = (values - high.astype(F32)).astype(BF16)
    return high, low


def level_of(steps_ref):
    return (steps_ref[0].astype(F32) + 1.0) * (1.0 / (STEPS + 1.0))


def time_embedding(step_value, width):
    half_width = width // 2
    ranks = lax.broadcasted_iota(jnp.int32, (1, half_width), 1).astype(F32) / half_width
    phases = step_value * jnp.exp(-math.log(10000.0) * ranks)
    return jnp.concatenate([jnp.cos(phases), jnp.sin(phases)], axis=1)


def scaled_and_rms(features, gain):
    features_f = features.astype(F32)
    mean_square = jnp.sum(features_f * features_f, axis=1, keepdims=True) / features.shape[1]
    return (features_f * gain).astype(BF16), lax.rsqrt(mean_square + 1e-06)


def latents_kernel(steps_ref, features_hbm, gain_hbm, weight_hbm, noise_hbm, send_ref, features, gain, weight, noise, sems):
    half = lax.axis_index("mp") // 2
    tokens, width = features.shape
    part = tokens // 2
    copies = [
        pltpu.make_async_copy(gain_hbm, gain, sems.at[4]),
        pltpu.make_async_copy(weight_hbm, weight, sems.at[5]),
        pltpu.make_async_copy(noise_hbm, noise, sems.at[6]),
    ]
    halves = []
    for i in range(2):
        start = pl.multiple_of(((half + i) % 2) * part, part)
        rows = features.at[pl.ds(i * part, part), :]
        halves.append(pltpu.make_async_copy(features_hbm.at[pl.ds(start, part), :], rows, sems.at[i]))
    for copy in copies[:1] + halves + copies[1:]:
        copy.start()
    level = level_of(steps_ref)
    copies[0].wait()
    gain_row = gain[...].astype(F32).reshape(1, width)
    scaled, inverse = [], []
    for i in range(2):
        halves[i].wait()
        one, inv_rms = scaled_and_rms(features[i * part : (i + 1) * part, :], gain_row)
        scaled.append(one)
        inverse.append(inv_rms)
    inv_row = jnp.broadcast_to(jnp.concatenate(inverse, axis=0), (tokens, tokens)).T[0:1]
    copies[1].wait()
    clean = dot(weight[...], jnp.concatenate(scaled, axis=0), NT) * inv_row
    copies[2].wait()
    noise_here = pltpu.roll(noise[...].astype(F32), (tokens - half * part) % tokens, 1)
    rounded = ((1.0 - level) * clean + level * noise_here).astype(BF16)
    for target in range(send_ref.shape[0]):
        send_ref[target] = rounded


def own_kernel(steps_ref, features_hbm, gain_hbm, weight_hbm, noise_hbm, picked_ref, own_ref, inv_ref, features, gain, weight, noise, turned, sems):
    slot = lax.axis_index("mp")
    width = features.shape[1]
    pairs = ((gain_hbm, gain), (features_hbm, features), (weight_hbm, weight), (noise_hbm, noise))
    copies = [pltpu.make_async_copy(source, target, sems.at[i]) for i, (source, target) in enumerate(pairs)]
    for copy in copies:
        copy.start()
    for copy in copies:
        copy.wait()
    level = level_of(steps_ref)
    scaled, inv_rms = scaled_and_rms(features[...], gain[...].astype(F32).reshape(1, width))
    inv_row = jnp.broadcast_to(inv_rms, (128, 128)).T[0:1]
    inv_ref[...] = jnp.broadcast_to(inv_row, inv_ref.shape)
    clean = dot(weight[...], scaled, NT) * inv_row
    own_ref[0:64, :] = clean
    own_ref[64:128, :] = (1.0 - level) * clean + level * noise[...].astype(F32)
    turned[...] = scaled.T
    for s in range(16):
        start = pl.multiple_of(s * 192 + slot * 48, 16)
        picked_ref[s * 48 : (s + 1) * 48, :] = turned[pl.ds(start, 48), :]


def fold_kernel(steps_ref, embed_hbm, gain_hbm, qkv_hbm, qk_hbm, out_hbm, fold_ref, scale_ref, embed, gain, qkv, qk, out, sems):
    model = lax.axis_index("mp") % 2
    head = lax.axis_index("seq")
    width = embed.shape[1]
    parts = 3
    chunk = width // parts
    columns = pl.ds(pl.multiple_of(head * 128, 128), 128)
    pairs = ((embed_hbm.at[model], embed), (gain_hbm, gain), (qk_hbm.at[model], qk), (out_hbm.at[model, :, columns], out))
    copies = [pltpu.make_async_copy(source, target, sems.at[i]) for i, (source, target) in enumerate(pairs)]
    pieces = []
    for k in range(parts):
        span = pl.ds(k * chunk, chunk)
        pieces.append(pltpu.make_async_copy(qkv_hbm.at[model, :, span, :], qkv.at[:, span, :], sems.at[4 + k]))
    for copy in copies + pieces:
        copy.start()
    temb = time_embedding(steps_ref[0].astype(F32), width)
    squares = jnp.sum(temb * temb, axis=1, keepdims=True)
    spot = lax.broadcasted_iota(jnp.int32, (16, width), 0)
    temb_one = temb.astype(BF16).astype(F32)
    temb_two = (temb - temb_one).astype(BF16).astype(F32)
    temb_three = temb - temb_one - temb_two
    temb_rows = jnp.where(spot == 0, temb_one, jnp.where(spot == 1, temb_two, jnp.where(spot == 2, temb_three, 0.0))).astype(BF16)
    for copy in copies:
        copy.wait()
    gain_row = jnp.where(model == 0, gain[0:1, :].astype(F32), gain[1:2, :].astype(F32))
    table = embed[...]
    high, low = split_two(table.astype(F32) * gain_row)
    biased = temb * gain_row
    bias_high = biased.astype(BF16).astype(F32)
    bias_rows = jnp.where(spot == 0, bias_high, jnp.where(spot == 1, biased - bias_high, 0.0)).astype(BF16)
    rows = jnp.concatenate([high, low, bias_rows], axis=0)
    pads = jnp.zeros((48, width), BF16)
    inner = dot(table, jnp.concatenate([table, temb_rows, pads], axis=0), NT)
    acc = jnp.zeros((144, 384), F32)
    for k in range(parts):
        pieces[k].wait()
        span = slice(k * chunk, (k + 1) * chunk)
        acc += dot(rows[:, span], jnp.concatenate([qkv[i, span, :] for i in range(3)], axis=1))
    lane = lax.broadcasted_iota(jnp.int32, (64, 128), 1)
    row = lax.broadcasted_iota(jnp.int32, (64, 128), 0)

    def stacked(i):
        whole = acc[:, i * 128 : (i + 1) * 128]
        bias = whole[128:129] + whole[129:130]
        return jnp.concatenate([whole[0:64] + whole[64:128], jnp.where(row == 0, bias, 0.0)], axis=0)

    value_high, value_low = split_two(stacked(2))
    mixed = dot(out[...], value_high, NT) + dot(out[...], value_low, NT)
    linear = inner[:, 64:65] + inner[:, 65:66] + inner[:, 66:67]
    inner = jnp.where(lane < 64, inner, jnp.where(lane == 64, 2.0 * linear, 0.0))
    high, low = split_two(jnp.concatenate([stacked(1).T, mixed, inner, stacked(0).T], axis=0))
    fold_ref[...] = jnp.concatenate([high, low], axis=1)
    gains = qk[0:1, :].astype(F32) * qk[1:2, :].astype(F32) * (math.log2(math.e) / math.sqrt(128.0))
    scale_ref[0:128, :] = jnp.broadcast_to(gains, (128, 128)).T
    scale_ref[128:136, :] = jnp.broadcast_to(squares, (8, 128))


def packed(block, odd):
    left = lax.broadcasted_iota(jnp.int32, (32, 128), 1) < 64
    if odd:
        return jnp.where(left, pltpu.roll(block[0:32], 64, 1), block[32:64])
    return jnp.where(left, block[0:32], pltpu.roll(block[32:64], 64, 1))


def attention_kernel(latent_hbm, fold_hbm, scale_hbm, send_ref, latent_ref, fold_ref, scale_ref, latents, queries, sems):
    pairs = ((latent_hbm, latent_ref), (fold_hbm, fold_ref), (scale_hbm, scale_ref))
    copies = [pltpu.make_async_copy(source, target, sems.at[i]) for i, (source, target) in enumerate(pairs)]
    for copy in copies:
        copy.start()
    blocks = latent_ref.shape[0]
    keys = blocks * 128
    count = blocks * 64
    for table in (latents, queries):
        table[64:128, :] = jnp.ones((64, table.shape[1]), BF16)
        table[192:256, :] = jnp.ones((64, table.shape[1]), BF16)
    copies[0].wait()
    for s in range(blocks):
        block = latent_ref[s]
        latents[0:64, s * 128 : (s + 1) * 128] = block
        latents[128:192, s * 128 : (s + 1) * 128] = block
    for g in range(blocks // 2):
        pieces = jnp.concatenate([latent_ref[2 * g + i][:, 0:64] for i in range(2)], axis=1)
        queries[0:64, g * 128 : (g + 1) * 128] = pieces
        queries[128:192, g * 128 : (g + 1) * 128] = pieces
    for copy in copies[1:]:
        copy.wait()
    squares = scale_ref[128:129, 0:1]

    def hidden_square(inner, rows):
        return (jnp.sum(inner * rows.astype(F32), axis=0, keepdims=True) + squares) / 3072.0 + 1e-06

    projected = dot(fold_ref[0:256], latents[...])
    hidden = hidden_square(projected[192:256], latents[0:64])
    key = projected[0:128]
    key_scale = lax.rsqrt(jnp.mean(key * key, axis=0, keepdims=True) + 1e-06 * hidden)
    key = (key * key_scale).astype(BF16).T
    value = (projected[128:192] * lax.rsqrt(hidden)).astype(BF16)
    value = jnp.concatenate([value, jnp.ones((16, keys), BF16)], axis=0)
    projected = dot(fold_ref[192:384], queries[...])
    hidden = hidden_square(projected[0:64], queries[0:64])
    query = projected[64:192]
    query_scale = lax.rsqrt(jnp.mean(query * query, axis=0, keepdims=True) + 1e-06 * hidden)
    query = query * query_scale * jnp.concatenate([scale_ref[0:128]] * (count // 128), axis=1)
    query = query.astype(BF16)
    total = jnp.zeros((80, count), F32)
    step = 512
    for c in range(keys // step):
        span = slice(c * step, (c + 1) * step)
        shares = jnp.exp2(dot(key[span], query)).astype(BF16)
        total += dot(value[:, span], shares)
    mixed = total[0:64] / total[64:65]
    for s in range(blocks):
        send_ref[s] = packed(mixed[:, (s // 2) * 128 : (s // 2 + 1) * 128], s % 2).astype(BF16)


def sum_kernel(part_ref, send_ref):
    send_ref[...] = jnp.sum(part_ref[...].astype(F32), axis=0)


def gap_kernel(steps_ref, zero_ref, one_ref, two_ref, three_ref, picked_ref, own_ref, inv_ref, send_ref, gap_ref, every):
    level = level_of(steps_ref)
    blocks = send_ref.shape[0]
    slot = lax.axis_index("mp")
    for k, ref in enumerate((zero_ref, one_ref, two_ref, three_ref)):
        every[slot ^ k] = ref[...]
    left = lax.broadcasted_iota(jnp.int32, (64, 128), 1) < 64

    def velocity(model):
        first, second = every[model], every[model + 2]
        first = jnp.concatenate([first, pltpu.roll(first, 64, 1)], axis=0)
        second = jnp.concatenate([pltpu.roll(second, 64, 1), second], axis=0)
        return jnp.where(left, first, second)

    teacher = velocity(0)
    gap = level * (teacher - velocity(1))
    gap_ref[...] = gap
    distance = jnp.abs(own_ref[0:64] - (own_ref[64:128] - level * teacher))
    spread = jnp.sum(jnp.sum(distance, axis=1, keepdims=True), axis=0, keepdims=True)
    direction = (gap * inv_ref[0:1]).astype(BF16)
    grad = dot(picked_ref[...], jnp.concatenate([direction, direction], axis=0), NT)
    spread = jnp.broadcast_to(spread, (8, 128))
    spot = lax.broadcasted_iota(jnp.int32, (8, 128), 0)
    high = spread.astype(BF16).astype(F32)
    tail = jnp.where(spot == 0, high, jnp.where(spot == 1, spread - high, 0.0))
    left = lax.broadcasted_iota(jnp.int32, (24, 128), 1) < 64
    for s in range(blocks):
        packed = jnp.where(left, grad[s * 48 : s * 48 + 24], grad[s * 48 + 24 : s * 48 + 48])
        send_ref[s] = jnp.concatenate([packed, tail], axis=0).astype(BF16)


def weight_inverse(total):
    return 1.0 / ((total[24:25] + total[25:26]) / 131072.0 + 1e-05)


def total_kernel(grad_ref, send_ref, inverse_ref):
    total = jnp.sum(grad_ref[...].astype(F32), axis=0)
    inverse = weight_inverse(total)
    inverse_ref[...] = jnp.broadcast_to(inverse, inverse_ref.shape)
    whole = (total[0:24] * inverse).astype(BF16)
    for target in range(send_ref.shape[0]):
        send_ref[target] = whole


def result_kernel(all_ref, gap_ref, inverse_ref, dmd_ref, grad_ref):
    dmd_ref[...] = gap_ref[...] * inverse_ref[0:1]
    rows = []
    for m in range(4):
        total = jnp.sum(all_ref[4 * m : 4 * m + 4].astype(F32), axis=0)
        rows += [total, pltpu.roll(total, 64, 1)]
    rows.append(jnp.zeros((64, 128), F32))
    grad_ref[...] = jnp.concatenate(rows, axis=0).T[0:64, 0:192]


def call(kernel, outs, in_specs, name, flops=0, moved=0, grant=32, **more):
    return pl.pallas_call(
        kernel,
        out_shape=outs,
        in_specs=in_specs,
        out_specs=more.pop("out_specs", jax.tree.map(lambda _: VMEM, outs)),
        compiler_params=pltpu.CompilerParams(vmem_limit_bytes=grant * MEBI),
        cost_estimate=pl.CostEstimate(flops=flops, bytes_accessed=moved, transcendentals=0),
        name=name,
        **more,
    )


def per_device(
    gen_features,
    gen_gain,
    gen_weight,
    flow_noise,
    time_steps,
    embed_weight,
    norm_gain,
    qkv_weight,
    qk_gain,
    out_weight,
):
    shape = jax.ShapeDtypeStruct
    seq_count = lax.axis_size("seq")
    group = lax.axis_size("mp") * lax.axis_size("dp")
    features = gen_features[0]
    tokens, width = features.shape
    local = (time_steps, features, gen_gain, gen_weight.T, flow_noise[0].T)
    buffers = [
        pltpu.VMEM((tokens, width), BF16),
        pltpu.VMEM((width,), BF16),
        pltpu.VMEM((64, width), BF16),
        pltpu.VMEM((64, tokens), BF16),
    ]
    send = call(
        latents_kernel,
        shape((seq_count, 64, tokens), BF16),
        [SMEM] + [HBM] * 4,
        "latents",
        grant=60,
        flops=2 * tokens * width * 64,
        moved=2 * tokens * width,
        scratch_shapes=buffers + [pltpu.SemaphoreType.DMA((7,))],
    )(*local)
    every_latent = lax.all_to_all(send, "seq", 0, 0)

    fold, scale = call(
        fold_kernel,
        (shape((384, 256), BF16), shape((136, 128), F32)),
        [SMEM] + [HBM] * 5,
        "fold",
        grant=60,
        flops=2 * width * 384 * 256,
        moved=2 * width * 384,
        scratch_shapes=[
            pltpu.VMEM((64, width), BF16),
            pltpu.VMEM((2, width), BF16),
            pltpu.VMEM((3, width, 128), BF16),
            pltpu.VMEM((2, 128), BF16),
            pltpu.VMEM((64, 128), BF16),
            pltpu.SemaphoreType.DMA((7,)),
        ],
    )(
        time_steps,
        embed_weight,
        norm_gain,
        qkv_weight.transpose(0, 2, 1, 3),
        qk_gain,
        out_weight.transpose(0, 2, 1),
    )
    keys = seq_count * tokens
    send = call(
        attention_kernel,
        shape((seq_count, 32, 128), BF16),
        [HBM] * 3,
        "attention",
        grant=60,
        flops=2 * keys * (keys // 2) * 256,
        moved=2 * keys * 64,
        scratch_shapes=[
            pltpu.VMEM((seq_count, 64, tokens), BF16),
            pltpu.VMEM((384, 256), BF16),
            pltpu.VMEM((136, 128), F32),
            pltpu.VMEM((256, keys), BF16),
            pltpu.VMEM((256, keys // 2), BF16),
            pltpu.SemaphoreType.DMA((3,)),
        ],
    )(every_latent, fold, scale)
    every_part = lax.all_to_all(send, "seq", 0, 0)
    send = call(sum_kernel, shape((32, 128), F32), [VMEM], "sum", moved=2 * seq_count * 32 * 128)(every_part)
    velocities = [send] + [lax.ppermute(send, "mp", [(i, i ^ k) for i in range(4)]) for k in range(1, 4)]
    picked, own, inv = call(
        own_kernel,
        (shape((width // 4, tokens), BF16), shape((128, tokens), F32), shape((8, tokens), F32)),
        [SMEM] + [HBM] * 4,
        "own",
        flops=2 * tokens * width * 64,
        moved=2 * tokens * width,
        scratch_shapes=buffers + [pltpu.VMEM((width, tokens), BF16), pltpu.SemaphoreType.DMA((4,))],
    )(*local)
    send, gap = call(
        gap_kernel,
        (shape((seq_count, 32, 128), BF16), shape((64, tokens), F32)),
        [SMEM] + [VMEM] * 7,
        "gap",
        flops=2 * tokens * width * 16,
        moved=2 * 64 * 32 * 128,
        scratch_shapes=[pltpu.VMEM((4, 32, 128), F32)],
    )(time_steps, *velocities, picked, own, inv)
    partials = lax.all_to_all(send, "seq", 0, 0)
    send, inverse = call(
        total_kernel,
        (shape((group, 24, 128), BF16), shape((8, 128), F32)),
        [VMEM],
        "total",
        flops=seq_count * 32 * 128,
        moved=2 * seq_count * 32 * 128,
    )(partials)
    every_total = lax.all_to_all(send, ("mp", "dp"), 0, 0)
    dmd, grad = call(
        result_kernel,
        (shape((64, tokens), F32), shape((64, width // seq_count), F32)),
        [VMEM] * 3,
        "result",
        flops=group * 24 * 128,
        moved=2 * group * 24 * 128,
    )(every_total, gap, inverse)
    return dmd.T[None], grad.T


def solution(mesh):
    placed = (
        P("dp", "seq", None),
        P(),
        P(),
        P("dp", "seq", None),
        P("dp"),
        P(),
        P(),
        P(None, None, None, "seq"),
        P(),
        P(),
    )
    return jax.shard_map(
        per_device,
        mesh=mesh,
        in_specs=placed,
        out_specs=(P("dp", "seq", None), P("seq", None)),
        check_vma=False,
    )
```

```python
import math

import jax
import jax.numpy as jnp
from jax import lax
from jax.experimental import pallas as pl
from jax.experimental.pallas import tpu as pltpu
from jax.sharding import PartitionSpec as P

F32 = jnp.float32
BF16 = jnp.bfloat16
STEPS = 1000
NN = (((1,), (0,)), ((), ()))
NT = (((1,), (1,)), ((), ()))
TN = (((0,), (0,)), ((), ()))
VMEM = pl.BlockSpec(memory_space=pltpu.VMEM)
SMEM = pl.BlockSpec(memory_space=pltpu.SMEM)
HBM = pl.BlockSpec(memory_space=pltpu.HBM)
MEBI = 1024 * 1024


def dot(left, right, dims=NN):
    return lax.dot_general(left, right, dims, preferred_element_type=F32)


def split_two(values):
    high = values.astype(BF16)
    low = (values - high.astype(F32)).astype(BF16)
    return high, low


def place():
    slot = lax.axis_index("mp")
    half = slot // 2
    return slot, (slot + half) % 2, half


def slot_of(model, half):
    return 2 * half + (model + half) % 2


def level_of(steps_ref):
    return (steps_ref[0].astype(F32) + 1.0) * (1.0 / (STEPS + 1.0))


def time_embedding(step_value, width):
    half_width = width // 2
    ranks = lax.broadcasted_iota(jnp.int32, (1, half_width), 1).astype(F32) / half_width
    phases = step_value * jnp.exp(-math.log(10000.0) * ranks)
    return jnp.concatenate([jnp.cos(phases), jnp.sin(phases)], axis=1)


def scaled_and_rms(features, gain):
    features_f = features.astype(F32)
    mean_square = jnp.sum(features_f * features_f, axis=1, keepdims=True) / features.shape[1]
    return (features_f * gain).astype(BF16), lax.rsqrt(mean_square + 1e-06)


def latents_kernel(steps_ref, features_hbm, gain_hbm, weight_hbm, noise_hbm, send_ref, features, gain, weight, noise, sems):
    _, _, half = place()
    tokens, width = features.shape
    part = tokens // 2
    copies = [
        pltpu.make_async_copy(gain_hbm, gain, sems.at[0]),
        pltpu.make_async_copy(noise_hbm, noise, sems.at[2]),
    ]
    parts = 2
    chunk = width // parts
    pieces = []
    for k in range(parts):
        span = pl.ds(k * chunk, chunk)
        group = [pltpu.make_async_copy(weight_hbm.at[:, span], weight.at[:, span], sems.at[3 + 3 * k])]
        for i in range(2):
            start = pl.multiple_of(((half + i) % 2) * part, part)
            here = features.at[pl.ds(i * part, part), span]
            group.append(pltpu.make_async_copy(features_hbm.at[pl.ds(start, part), span], here, sems.at[4 + 3 * k + i]))
        pieces.append(group)
    for copy in copies[:1] + sum(pieces, []) + copies[1:]:
        copy.start()
    level = level_of(steps_ref)
    copies[0].wait()
    gain_row = gain[...].astype(F32).reshape(1, width)
    clean = jnp.zeros((64, tokens), F32)
    squares = jnp.zeros((tokens, 128), F32)
    for k in range(parts):
        for copy in pieces[k]:
            copy.wait()
        span = slice(k * chunk, (k + 1) * chunk)
        values = features[:, span].astype(F32)
        for j in range(chunk // 128):
            one = values[:, j * 128 : (j + 1) * 128]
            squares += one * one
        clean += dot(weight[:, span], (values * gain_row[:, span]).astype(BF16), NT)
    mean_square = jnp.sum(squares, axis=1, keepdims=True) / width
    inv_row = lax.rsqrt(jnp.broadcast_to(mean_square, (tokens, tokens)).T[0:1] + 1e-06)
    clean = clean * inv_row
    copies[1].wait()
    noise_here = pltpu.roll(noise[...].astype(F32), (tokens - half * part) % tokens, 1)
    rounded = ((1.0 - level) * clean + level * noise_here).astype(BF16)
    for target in range(send_ref.shape[0]):
        send_ref[target] = rounded


def own_kernel(steps_ref, features_hbm, gain_hbm, weight_hbm, noise_hbm, picked_ref, own_ref, features, gain, weight, noise, turned, sems):
    _, model, half = place()
    width = features.shape[1]
    pairs = ((gain_hbm, gain), (features_hbm, features), (weight_hbm, weight), (noise_hbm, noise))
    copies = [pltpu.make_async_copy(source, target, sems.at[i]) for i, (source, target) in enumerate(pairs)]
    for copy in copies:
        copy.start()
    for copy in copies:
        copy.wait()
    level = level_of(steps_ref)
    scaled, inv_rms = scaled_and_rms(features[...], gain[...].astype(F32).reshape(1, width))
    inv_row = jnp.broadcast_to(inv_rms, (128, 128)).T[0:1]
    clean = dot(weight[...], scaled, NT) * inv_row
    noisy = (1.0 - level) * clean + level * noise[...].astype(F32)
    first = half == 0
    own_ref[0:32, :] = jnp.where(first, packed(clean, 0), packed(clean, 1))
    own_ref[32:64, :] = jnp.where(first, packed(noisy, 0), packed(noisy, 1))
    inverse = jnp.broadcast_to(inv_row, (8, 128))
    left = lax.broadcasted_iota(jnp.int32, (8, 128), 1) < 64
    turned_row = pltpu.roll(inverse, 64, 1)
    own_ref[64:72, :] = jnp.where(left, jnp.where(first, inverse, turned_row), jnp.where(first, turned_row, inverse))
    turned[...] = scaled.T
    for s in range(16):
        start = pl.multiple_of(s * 192 + model * 96, 32)
        picked_ref[s * 96 : (s + 1) * 96, :] = turned[pl.ds(start, 96), :]


def fold_kernel(steps_ref, embed_hbm, gain_hbm, qkv_hbm, qk_hbm, out_hbm, fold_ref, scale_ref, embed, gain, qkv, qk, out, sems):
    _, model, _ = place()
    head = lax.axis_index("seq")
    width = embed.shape[1]
    parts = 3
    chunk = width // parts
    columns = pl.ds(pl.multiple_of(head * 128, 128), 128)
    pairs = ((embed_hbm.at[model], embed), (gain_hbm, gain), (qk_hbm.at[model], qk), (out_hbm.at[model, :, columns], out))
    copies = [pltpu.make_async_copy(source, target, sems.at[i]) for i, (source, target) in enumerate(pairs)]
    pieces = []
    for k in range(parts):
        span = pl.ds(k * chunk, chunk)
        pieces.append(pltpu.make_async_copy(qkv_hbm.at[model, :, span, :], qkv.at[:, span, :], sems.at[4 + k]))
    for copy in copies + pieces:
        copy.start()
    temb = time_embedding(steps_ref[0].astype(F32), width)
    squares = jnp.sum(temb * temb, axis=1, keepdims=True)
    spot = lax.broadcasted_iota(jnp.int32, (16, width), 0)
    temb_one = temb.astype(BF16).astype(F32)
    temb_two = (temb - temb_one).astype(BF16).astype(F32)
    temb_three = temb - temb_one - temb_two
    temb_rows = jnp.where(spot == 0, temb_one, jnp.where(spot == 1, temb_two, jnp.where(spot == 2, temb_three, 0.0))).astype(BF16)
    for copy in copies:
        copy.wait()
    gain_row = jnp.where(model == 0, gain[0:1, :].astype(F32), gain[1:2, :].astype(F32))
    table = embed[...]
    high, low = split_two(table.astype(F32) * gain_row)
    biased = temb * gain_row
    bias_high = biased.astype(BF16).astype(F32)
    bias_rows = jnp.where(spot == 0, bias_high, jnp.where(spot == 1, biased - bias_high, 0.0)).astype(BF16)
    rows = jnp.concatenate([high, low, bias_rows], axis=0)
    pads = jnp.zeros((48, width), BF16)
    inner = dot(table, jnp.concatenate([table, temb_rows, pads], axis=0), NT)
    acc = jnp.zeros((144, 384), F32)
    for k in range(parts):
        pieces[k].wait()
        span = slice(k * chunk, (k + 1) * chunk)
        acc += dot(rows[:, span], jnp.concatenate([qkv[i, span, :] for i in range(3)], axis=1))
    lane = lax.broadcasted_iota(jnp.int32, (64, 128), 1)
    row = lax.broadcasted_iota(jnp.int32, (64, 128), 0)

    def stacked(i):
        whole = acc[:, i * 128 : (i + 1) * 128]
        bias = whole[128:129] + whole[129:130]
        return jnp.concatenate([whole[0:64] + whole[64:128], jnp.where(row == 0, bias, 0.0)], axis=0)

    value_high, value_low = split_two(stacked(2))
    mixed = dot(out[...], value_high, NT) + dot(out[...], value_low, NT)
    linear = inner[:, 64:65] + inner[:, 65:66] + inner[:, 66:67]
    inner = jnp.where(lane < 64, inner, jnp.where(lane == 64, 2.0 * linear, 0.0))
    high, low = split_two(jnp.concatenate([stacked(1).T, mixed, inner, stacked(0).T], axis=0))
    fold_ref[...] = jnp.concatenate([high, low], axis=1)
    gains = qk[0:1, :].astype(F32) * qk[1:2, :].astype(F32) * (math.log2(math.e) / math.sqrt(128.0))
    scale_ref[0:128, :] = jnp.broadcast_to(gains, (128, 128)).T
    scale_ref[128:136, :] = jnp.broadcast_to(squares, (8, 128))


def packed(block, odd):
    left = lax.broadcasted_iota(jnp.int32, (32, 128), 1) < 64
    if odd:
        return jnp.where(left, pltpu.roll(block[0:32], 64, 1), block[32:64])
    return jnp.where(left, block[0:32], pltpu.roll(block[32:64], 64, 1))


def attention_kernel(latent_hbm, fold_hbm, scale_hbm, send_ref, latent_ref, fold_ref, scale_ref, latents, queries, sems):
    pairs = ((latent_hbm, latent_ref), (fold_hbm, fold_ref), (scale_hbm, scale_ref))
    copies = [pltpu.make_async_copy(source, target, sems.at[i]) for i, (source, target) in enumerate(pairs)]
    for copy in copies:
        copy.start()
    blocks = latent_ref.shape[0]
    keys = blocks * 128
    count = blocks * 64
    for table in (latents, queries):
        table[64:128, :] = jnp.ones((64, table.shape[1]), BF16)
        table[192:256, :] = jnp.ones((64, table.shape[1]), BF16)
    copies[0].wait()
    for s in range(blocks):
        block = latent_ref[s]
        latents[0:64, s * 128 : (s + 1) * 128] = block
        latents[128:192, s * 128 : (s + 1) * 128] = block
    for g in range(blocks // 2):
        pieces = jnp.concatenate([latent_ref[2 * g + i][:, 0:64] for i in range(2)], axis=1)
        queries[0:64, g * 128 : (g + 1) * 128] = pieces
        queries[128:192, g * 128 : (g + 1) * 128] = pieces
    for copy in copies[1:]:
        copy.wait()
    squares = scale_ref[128:129, 0:1]

    def hidden_square(inner, rows):
        return (jnp.sum(inner * rows.astype(F32), axis=0, keepdims=True) + squares) / 3072.0 + 1e-06

    projected = dot(fold_ref[0:256], latents[...])
    hidden = hidden_square(projected[192:256], latents[0:64])
    key = projected[0:128]
    key_scale = lax.rsqrt(jnp.mean(key * key, axis=0, keepdims=True) + 1e-06 * hidden)
    key = (key * key_scale).astype(BF16).T
    value = (projected[128:192] * lax.rsqrt(hidden)).astype(BF16)
    value = jnp.concatenate([value, jnp.ones((16, keys), BF16)], axis=0)
    projected = dot(fold_ref[192:384], queries[...])
    hidden = hidden_square(projected[0:64], queries[0:64])
    query = projected[64:192]
    query_scale = lax.rsqrt(jnp.mean(query * query, axis=0, keepdims=True) + 1e-06 * hidden)
    query = query * query_scale * jnp.concatenate([scale_ref[0:128]] * (count // 128), axis=1)
    query = query.astype(BF16)
    total = jnp.zeros((80, count), F32)
    step = 512
    for c in range(keys // step):
        span = slice(c * step, (c + 1) * step)
        shares = jnp.exp2(dot(key[span], query)).astype(BF16)
        total += dot(value[:, span], shares)
    mixed = total[0:64] / total[64:65]
    for s in range(blocks):
        block = packed(mixed[:, (s // 2) * 128 : (s // 2 + 1) * 128], s % 2).astype(BF16)
        send_ref[s] = block
        send_ref[blocks + s] = block


def gap_kernel(steps_ref, velocity_ref, picked_ref, own_ref, send_ref, gap_ref):
    level = level_of(steps_ref)
    _, _, half = place()
    teacher = jnp.sum(velocity_ref[0:16].astype(F32), axis=0)
    gap = level * (teacher - jnp.sum(velocity_ref[16:32].astype(F32), axis=0))
    gap_ref[...] = gap
    distance = jnp.abs(own_ref[0:32] - (own_ref[32:64] - level * teacher))
    spread = jnp.sum(jnp.sum(distance, axis=1, keepdims=True), axis=0, keepdims=True)
    direction = gap * own_ref[64:65]
    turned = pltpu.roll(direction, 64, 1)
    left = lax.broadcasted_iota(jnp.int32, (64, 128), 1) < 64
    rows = jnp.where(
        half == 0,
        jnp.where(left, jnp.concatenate([direction, turned], axis=0), 0.0),
        jnp.where(left, 0.0, jnp.concatenate([turned, direction], axis=0)),
    ).astype(BF16)
    grad = dot(picked_ref[...], jnp.concatenate([rows, rows], axis=0), NT)
    tail = spread_rows(spread)
    left = left[0:48]
    for s in range(send_ref.shape[0]):
        pair = jnp.where(left, grad[s * 96 : s * 96 + 48], grad[s * 96 + 48 : s * 96 + 96])
        send_ref[s] = jnp.concatenate([pair, tail], axis=0).astype(BF16)


def spread_rows(spread):
    spread = jnp.broadcast_to(spread, (8, 128))
    spot = lax.broadcasted_iota(jnp.int32, (8, 128), 0)
    high = spread.astype(BF16).astype(F32)
    return jnp.where(spot == 0, high, jnp.where(spot == 1, spread - high, 0.0))


def total_kernel(grad_ref, send_ref):
    total = jnp.sum(grad_ref[...].astype(F32), axis=0)
    tail = spread_rows(total[48:49] + total[49:50])
    whole = jnp.concatenate([total[0:48], tail], axis=0).astype(BF16)
    for target in range(send_ref.shape[0]):
        send_ref[target] = whole


def result_kernel(all_ref, gap_ref, other_ref, dmd_ref, grad_ref):
    _, _, half = place()
    sample = lax.axis_index("dp")
    totals = [jnp.zeros((48, 128), F32)] * 2
    mine = jnp.zeros((1, 128), F32)
    for d in range(4):
        sums = [sum(all_ref[4 * slot_of(m, h) + d].astype(F32) for h in range(2)) for m in range(2)]
        inverse = 1.0 / ((sums[0][48:49] + sums[0][49:50]) / 131072.0 + 1e-05)
        mine = jnp.where(sample == d, inverse, mine)
        totals = [total + one[0:48] * inverse for total, one in zip(totals, sums)]
    own = gap_ref[...] * mine
    other = other_ref[...] * mine
    first = jnp.where(half == 0, own, other)
    second = jnp.where(half == 0, other, own)
    left = lax.broadcasted_iota(jnp.int32, (32, 128), 1) < 64
    dmd_ref[0:32, :] = jnp.where(left, first, pltpu.roll(second, 64, 1))
    dmd_ref[32:64, :] = jnp.where(left, pltpu.roll(first, 64, 1), second)
    rows = []
    for total in totals:
        rows += [total, pltpu.roll(total, 64, 1)]
    rows.append(jnp.zeros((64, 128), F32))
    grad_ref[...] = jnp.concatenate(rows, axis=0).T[0:64, 0:192]


def call(kernel, outs, in_specs, name, flops=0, moved=0, grant=32, **more):
    return pl.pallas_call(
        kernel,
        out_shape=outs,
        in_specs=in_specs,
        out_specs=more.pop("out_specs", jax.tree.map(lambda _: VMEM, outs)),
        compiler_params=pltpu.CompilerParams(vmem_limit_bytes=grant * MEBI),
        cost_estimate=pl.CostEstimate(flops=flops, bytes_accessed=moved, transcendentals=0),
        name=name,
        **more,
    )


def pairs_of(seq_count):
    return [[slot_of(m, half) * seq_count + s for m in range(2) for s in range(seq_count)] for half in range(2)]


def per_device(
    gen_features,
    gen_gain,
    gen_weight,
    flow_noise,
    time_steps,
    embed_weight,
    norm_gain,
    qkv_weight,
    qk_gain,
    out_weight,
):
    shape = jax.ShapeDtypeStruct
    seq_count = lax.axis_size("seq")
    group = lax.axis_size("mp") * lax.axis_size("dp")
    features = gen_features[0]
    tokens, width = features.shape
    local = (time_steps, features, gen_gain, gen_weight.T, flow_noise[0].T)
    buffers = [
        pltpu.VMEM((tokens, width), BF16),
        pltpu.VMEM((width,), BF16),
        pltpu.VMEM((64, width), BF16),
        pltpu.VMEM((64, tokens), BF16),
    ]
    send = call(
        latents_kernel,
        shape((seq_count, 64, tokens), BF16),
        [SMEM] + [HBM] * 4,
        "latents",
        grant=63,
        flops=2 * tokens * width * 64,
        moved=2 * tokens * width,
        scratch_shapes=buffers + [pltpu.SemaphoreType.DMA((9,))],
    )(*local)
    every_latent = lax.all_to_all(send, "seq", 0, 0)

    fold, scale = call(
        fold_kernel,
        (shape((384, 256), BF16), shape((136, 128), F32)),
        [SMEM] + [HBM] * 5,
        "fold",
        grant=63,
        flops=2 * width * 384 * 256,
        moved=2 * width * 384,
        scratch_shapes=[
            pltpu.VMEM((64, width), BF16),
            pltpu.VMEM((2, width), BF16),
            pltpu.VMEM((3, width, 128), BF16),
            pltpu.VMEM((2, 128), BF16),
            pltpu.VMEM((64, 128), BF16),
            pltpu.SemaphoreType.DMA((7,)),
        ],
    )(
        time_steps,
        embed_weight,
        norm_gain,
        qkv_weight.transpose(0, 2, 1, 3),
        qk_gain,
        out_weight.transpose(0, 2, 1),
    )
    keys = seq_count * tokens
    send = call(
        attention_kernel,
        shape((2 * seq_count, 32, 128), BF16),
        [HBM] * 3,
        "attention",
        grant=63,
        flops=2 * keys * (keys // 2) * 256,
        moved=2 * keys * 64,
        scratch_shapes=[
            pltpu.VMEM((seq_count, 64, tokens), BF16),
            pltpu.VMEM((384, 256), BF16),
            pltpu.VMEM((136, 128), F32),
            pltpu.VMEM((256, keys), BF16),
            pltpu.VMEM((256, keys // 2), BF16),
            pltpu.SemaphoreType.DMA((3,)),
        ],
    )(every_latent, fold, scale)
    whole = ("mp", "seq")
    velocities = lax.all_to_all(send, whole, 0, 0, axis_index_groups=pairs_of(seq_count))
    picked, own = call(
        own_kernel,
        (shape((width // 2, tokens), BF16), shape((72, tokens), F32)),
        [SMEM] + [HBM] * 4,
        "own",
        flops=2 * tokens * width * 64,
        moved=2 * tokens * width,
        scratch_shapes=buffers + [pltpu.VMEM((width, tokens), BF16), pltpu.SemaphoreType.DMA((4,))],
    )(*local)
    send, gap = call(
        gap_kernel,
        (shape((seq_count, 56, 128), BF16), shape((32, 128), F32)),
        [SMEM] + [VMEM] * 3,
        "gap",
        flops=2 * tokens * width * 16,
        moved=2 * 64 * 32 * 128,
    )(time_steps, velocities, picked, own)
    other = lax.ppermute(gap, "mp", [(slot_of(m, h), slot_of(m, 1 - h)) for m in range(2) for h in range(2)])
    partials = lax.all_to_all(send, "seq", 0, 0)
    send = call(
        total_kernel,
        shape((group, 56, 128), BF16),
        [VMEM],
        "total",
        flops=seq_count * 56 * 128,
        moved=2 * seq_count * 56 * 128,
    )(partials)
    every_total = lax.all_to_all(send, ("mp", "dp"), 0, 0)
    dmd, grad = call(
        result_kernel,
        (shape((64, tokens), F32), shape((64, width // seq_count), F32)),
        [VMEM] * 3,
        "result",
        flops=group * 24 * 128,
        moved=2 * group * 24 * 128,
    )(every_total, gap, other)
    return dmd.T[None], grad.T


def solution(mesh):
    placed = (
        P("dp", "seq", None),
        P(),
        P(),
        P("dp", "seq", None),
        P("dp"),
        P(),
        P(),
        P(None, None, None, "seq"),
        P(),
        P(),
    )
    return jax.shard_map(
        per_device,
        mesh=mesh,
        in_specs=placed,
        out_specs=(P("dp", "seq", None), P("seq", None)),
        check_vma=False,
    )
```

```python
import math

import jax
import jax.numpy as jnp
from jax import lax
from jax.experimental import pallas as pl
from jax.experimental.pallas import tpu as pltpu
from jax.sharding import PartitionSpec as P

F32 = jnp.float32
BF16 = jnp.bfloat16
STEPS = 1000
NN = (((1,), (0,)), ((), ()))
NT = (((1,), (1,)), ((), ()))
TN = (((0,), (0,)), ((), ()))
VMEM = pl.BlockSpec(memory_space=pltpu.VMEM)
SMEM = pl.BlockSpec(memory_space=pltpu.SMEM)
HBM = pl.BlockSpec(memory_space=pltpu.HBM)
MEBI = 1024 * 1024


def dot(left, right, dims=NN):
    return lax.dot_general(left, right, dims, preferred_element_type=F32)


def split_two(values):
    high = values.astype(BF16)
    low = (values - high.astype(F32)).astype(BF16)
    return high, low


def place():
    slot = lax.axis_index("mp")
    half = slot // 2
    return slot, (slot + half) % 2, half


def slot_of(model, half):
    return 2 * half + (model + half) % 2


def level_of(steps_ref):
    return (steps_ref[0].astype(F32) + 1.0) * (1.0 / (STEPS + 1.0))


def time_embedding(step_value, width):
    half_width = width // 2
    ranks = lax.broadcasted_iota(jnp.int32, (1, half_width), 1).astype(F32) / half_width
    phases = step_value * jnp.exp(-math.log(10000.0) * ranks)
    return jnp.concatenate([jnp.cos(phases), jnp.sin(phases)], axis=1)


def scaled_and_rms(features, gain):
    features_f = features.astype(F32)
    mean_square = jnp.sum(features_f * features_f, axis=1, keepdims=True) / features.shape[1]
    return (features_f * gain).astype(BF16), lax.rsqrt(mean_square + 1e-06)


def latents_kernel(steps_ref, features_hbm, gain_hbm, weight_hbm, noise_hbm, send_ref, features, gain, weight, noise, sems):
    _, _, half = place()
    tokens, width = features.shape
    part = tokens // 2
    copies = [
        pltpu.make_async_copy(gain_hbm, gain, sems.at[0]),
        pltpu.make_async_copy(noise_hbm, noise, sems.at[2]),
    ]
    parts = 2
    chunk = width // parts
    pieces = []
    for k in range(parts):
        span = pl.ds(k * chunk, chunk)
        group = [pltpu.make_async_copy(weight_hbm.at[:, span], weight.at[:, span], sems.at[3 + 3 * k])]
        for i in range(2):
            start = pl.multiple_of(((half + i) % 2) * part, part)
            here = features.at[pl.ds(i * part, part), span]
            group.append(pltpu.make_async_copy(features_hbm.at[pl.ds(start, part), span], here, sems.at[4 + 3 * k + i]))
        pieces.append(group)
    for copy in copies[:1] + sum(pieces, []) + copies[1:]:
        copy.start()
    level = level_of(steps_ref)
    copies[0].wait()
    gain_row = gain[...].astype(F32).reshape(1, width)
    clean = jnp.zeros((64, tokens), F32)
    squares = jnp.zeros((tokens, 128), F32)
    for k in range(parts):
        for copy in pieces[k]:
            copy.wait()
        span = slice(k * chunk, (k + 1) * chunk)
        values = features[:, span].astype(F32)
        for j in range(chunk // 128):
            one = values[:, j * 128 : (j + 1) * 128]
            squares += one * one
        clean += dot(weight[:, span], (values * gain_row[:, span]).astype(BF16), NT)
    mean_square = jnp.sum(squares, axis=1, keepdims=True) / width
    inv_row = lax.rsqrt(jnp.broadcast_to(mean_square, (tokens, tokens)).T[0:1] + 1e-06)
    clean = clean * inv_row
    copies[1].wait()
    noise_here = pltpu.roll(noise[...].astype(F32), (tokens - half * part) % tokens, 1)
    rounded = ((1.0 - level) * clean + level * noise_here).astype(BF16)
    for target in range(send_ref.shape[0]):
        send_ref[target] = rounded


def own_kernel(steps_ref, features_hbm, gain_hbm, weight_hbm, noise_hbm, picked_ref, own_ref, features, gain, weight, noise, turned, sems):
    _, model, half = place()
    width = features.shape[1]
    pairs = ((gain_hbm, gain), (features_hbm, features), (weight_hbm, weight), (noise_hbm, noise))
    copies = [pltpu.make_async_copy(source, target, sems.at[i]) for i, (source, target) in enumerate(pairs)]
    for copy in copies:
        copy.start()
    for copy in copies:
        copy.wait()
    level = level_of(steps_ref)
    scaled, inv_rms = scaled_and_rms(features[...], gain[...].astype(F32).reshape(1, width))
    inv_row = jnp.broadcast_to(inv_rms, (128, 128)).T[0:1]
    clean = dot(weight[...], scaled, NT) * inv_row
    noisy = (1.0 - level) * clean + level * noise[...].astype(F32)
    first = half == 0
    own_ref[0:32, :] = jnp.where(first, packed(clean, 0), packed(clean, 1))
    own_ref[32:64, :] = jnp.where(first, packed(noisy, 0), packed(noisy, 1))
    inverse = jnp.broadcast_to(inv_row, (8, 128))
    left = lax.broadcasted_iota(jnp.int32, (8, 128), 1) < 64
    turned_row = pltpu.roll(inverse, 64, 1)
    own_ref[64:72, :] = jnp.where(left, jnp.where(first, inverse, turned_row), jnp.where(first, turned_row, inverse))
    turned[...] = scaled.T
    for s in range(16):
        start = pl.multiple_of(s * 192 + model * 96, 32)
        picked_ref[s * 96 : (s + 1) * 96, :] = turned[pl.ds(start, 96), :]


def fold_kernel(steps_ref, embed_hbm, gain_hbm, qkv_hbm, qk_hbm, out_hbm, fold_ref, scale_ref, embed, gain, qkv, qk, out, sems):
    _, model, _ = place()
    head = lax.axis_index("seq")
    width = embed.shape[1]
    parts = 3
    chunk = width // parts
    columns = pl.ds(pl.multiple_of(head * 128, 128), 128)
    pairs = ((embed_hbm.at[model], embed), (gain_hbm, gain), (qk_hbm.at[model], qk), (out_hbm.at[model, :, columns], out))
    copies = [pltpu.make_async_copy(source, target, sems.at[i]) for i, (source, target) in enumerate(pairs)]
    pieces = []
    for k in range(parts):
        span = pl.ds(k * chunk, chunk)
        pieces.append(pltpu.make_async_copy(qkv_hbm.at[model, :, span, :], qkv.at[:, span, :], sems.at[4 + k]))
    for copy in copies + pieces:
        copy.start()
    temb = time_embedding(steps_ref[0].astype(F32), width)
    squares = jnp.sum(temb * temb, axis=1, keepdims=True)
    spot = lax.broadcasted_iota(jnp.int32, (16, width), 0)
    temb_one = temb.astype(BF16).astype(F32)
    temb_two = (temb - temb_one).astype(BF16).astype(F32)
    temb_three = temb - temb_one - temb_two
    temb_rows = jnp.where(spot == 0, temb_one, jnp.where(spot == 1, temb_two, jnp.where(spot == 2, temb_three, 0.0))).astype(BF16)
    for copy in copies:
        copy.wait()
    gain_row = jnp.where(model == 0, gain[0:1, :].astype(F32), gain[1:2, :].astype(F32))
    table = embed[...]
    high, low = split_two(table.astype(F32) * gain_row)
    biased = temb * gain_row
    bias_high = biased.astype(BF16).astype(F32)
    bias_rows = jnp.where(spot == 0, bias_high, jnp.where(spot == 1, biased - bias_high, 0.0)).astype(BF16)
    rows = jnp.concatenate([high, low, bias_rows], axis=0)
    pads = jnp.zeros((48, width), BF16)
    inner = dot(table, jnp.concatenate([table, temb_rows, pads], axis=0), NT)
    acc = jnp.zeros((144, 384), F32)
    for k in range(parts):
        pieces[k].wait()
        span = slice(k * chunk, (k + 1) * chunk)
        acc += dot(rows[:, span], jnp.concatenate([qkv[i, span, :] for i in range(3)], axis=1))
    lane = lax.broadcasted_iota(jnp.int32, (64, 128), 1)
    row = lax.broadcasted_iota(jnp.int32, (64, 128), 0)

    def stacked(i):
        whole = acc[:, i * 128 : (i + 1) * 128]
        bias = whole[128:129] + whole[129:130]
        return jnp.concatenate([whole[0:64] + whole[64:128], jnp.where(row == 0, bias, 0.0)], axis=0)

    value_high, value_low = split_two(stacked(2))
    mixed = dot(out[...], value_high, NT) + dot(out[...], value_low, NT)
    linear = inner[:, 64:65] + inner[:, 65:66] + inner[:, 66:67]
    inner = jnp.where(lane < 64, inner, jnp.where(lane == 64, 2.0 * linear, 0.0))
    high, low = split_two(jnp.concatenate([stacked(1).T, mixed, inner, stacked(0).T], axis=0))
    fold_ref[...] = jnp.concatenate([high, low], axis=1)
    gains = qk[0:1, :].astype(F32) * qk[1:2, :].astype(F32) * (math.log2(math.e) / math.sqrt(128.0))
    scale_ref[0:128, :] = jnp.broadcast_to(gains, (128, 128)).T
    scale_ref[128:136, :] = jnp.broadcast_to(squares, (8, 128))


def packed(block, odd):
    left = lax.broadcasted_iota(jnp.int32, (32, 128), 1) < 64
    if odd:
        return jnp.where(left, pltpu.roll(block[0:32], 64, 1), block[32:64])
    return jnp.where(left, block[0:32], pltpu.roll(block[32:64], 64, 1))


def attention_kernel(latent_ref, fold_ref, scale_ref, send_ref, latents, queries):
    blocks = latent_ref.shape[0]
    keys = blocks * 128
    count = blocks * 64
    for table in (latents, queries):
        table[64:128, :] = jnp.ones((64, table.shape[1]), BF16)
        table[192:256, :] = jnp.ones((64, table.shape[1]), BF16)
    for s in range(blocks):
        block = latent_ref[s]
        latents[0:64, s * 128 : (s + 1) * 128] = block
        latents[128:192, s * 128 : (s + 1) * 128] = block
    for g in range(blocks // 2):
        pieces = jnp.concatenate([latent_ref[2 * g + i][:, 0:64] for i in range(2)], axis=1)
        queries[0:64, g * 128 : (g + 1) * 128] = pieces
        queries[128:192, g * 128 : (g + 1) * 128] = pieces
    squares = scale_ref[128:129, 0:1]

    def hidden_square(inner, rows):
        return (jnp.sum(inner * rows.astype(F32), axis=0, keepdims=True) + squares) / 3072.0 + 1e-06

    projected = dot(fold_ref[0:256], latents[...])
    hidden = hidden_square(projected[192:256], latents[0:64])
    key = projected[0:128]
    key_scale = lax.rsqrt(jnp.mean(key * key, axis=0, keepdims=True) + 1e-06 * hidden)
    key = (key * key_scale).astype(BF16).T
    value = (projected[128:192] * lax.rsqrt(hidden)).astype(BF16)
    value = jnp.concatenate([value, jnp.ones((16, keys), BF16)], axis=0)
    projected = dot(fold_ref[192:384], queries[...])
    hidden = hidden_square(projected[0:64], queries[0:64])
    query = projected[64:192]
    query_scale = lax.rsqrt(jnp.mean(query * query, axis=0, keepdims=True) + 1e-06 * hidden)
    query = query * query_scale * jnp.concatenate([scale_ref[0:128]] * (count // 128), axis=1)
    query = query.astype(BF16)
    total = jnp.zeros((80, count), F32)
    step = 512
    for c in range(keys // step):
        span = slice(c * step, (c + 1) * step)
        shares = jnp.exp2(dot(key[span], query)).astype(BF16)
        total += dot(value[:, span], shares)
    mixed = total[0:64] / total[64:65]
    for s in range(blocks):
        block = packed(mixed[:, (s // 2) * 128 : (s // 2 + 1) * 128], s % 2).astype(BF16)
        send_ref[s] = block
        send_ref[blocks + s] = block


def gap_kernel(steps_ref, velocity_ref, picked_ref, own_ref, send_ref, gap_ref):
    level = level_of(steps_ref)
    _, _, half = place()
    teacher = jnp.sum(velocity_ref[0:16].astype(F32), axis=0)
    gap = level * (teacher - jnp.sum(velocity_ref[16:32].astype(F32), axis=0))
    gap_ref[...] = gap
    distance = jnp.abs(own_ref[0:32] - (own_ref[32:64] - level * teacher))
    spread = jnp.sum(jnp.sum(distance, axis=1, keepdims=True), axis=0, keepdims=True)
    direction = gap * own_ref[64:65]
    turned = pltpu.roll(direction, 64, 1)
    left = lax.broadcasted_iota(jnp.int32, (64, 128), 1) < 64
    rows = jnp.where(
        half == 0,
        jnp.where(left, jnp.concatenate([direction, turned], axis=0), 0.0),
        jnp.where(left, 0.0, jnp.concatenate([turned, direction], axis=0)),
    ).astype(BF16)
    grad = dot(picked_ref[...], jnp.concatenate([rows, rows], axis=0), NT)
    tail = spread_rows(spread)
    left = left[0:48]
    for s in range(send_ref.shape[0]):
        pair = jnp.where(left, grad[s * 96 : s * 96 + 48], grad[s * 96 + 48 : s * 96 + 96])
        send_ref[s] = jnp.concatenate([pair, tail], axis=0).astype(BF16)


def spread_rows(spread):
    spread = jnp.broadcast_to(spread, (8, 128))
    spot = lax.broadcasted_iota(jnp.int32, (8, 128), 0)
    high = spread.astype(BF16).astype(F32)
    return jnp.where(spot == 0, high, jnp.where(spot == 1, spread - high, 0.0))


def total_kernel(grad_ref, send_ref):
    total = jnp.sum(grad_ref[...].astype(F32), axis=0)
    tail = spread_rows(total[48:49] + total[49:50])
    whole = jnp.concatenate([total[0:48], tail], axis=0).astype(BF16)
    for target in range(send_ref.shape[0]):
        send_ref[target] = whole


def result_kernel(all_ref, gap_ref, other_ref, dmd_ref, grad_ref):
    _, _, half = place()
    sample = lax.axis_index("dp")
    totals = [jnp.zeros((48, 128), F32)] * 2
    mine = jnp.zeros((1, 128), F32)
    for d in range(4):
        sums = [sum(all_ref[4 * slot_of(m, h) + d].astype(F32) for h in range(2)) for m in range(2)]
        inverse = 1.0 / ((sums[0][48:49] + sums[0][49:50]) / 131072.0 + 1e-05)
        mine = jnp.where(sample == d, inverse, mine)
        totals = [total + one[0:48] * inverse for total, one in zip(totals, sums)]
    own = gap_ref[...] * mine
    other = other_ref[...] * mine
    first = jnp.where(half == 0, own, other)
    second = jnp.where(half == 0, other, own)
    left = lax.broadcasted_iota(jnp.int32, (32, 128), 1) < 64
    dmd_ref[0:32, :] = jnp.where(left, first, pltpu.roll(second, 64, 1))
    dmd_ref[32:64, :] = jnp.where(left, pltpu.roll(first, 64, 1), second)
    rows = []
    for total in totals:
        rows += [total, pltpu.roll(total, 64, 1)]
    rows.append(jnp.zeros((64, 128), F32))
    grad_ref[...] = jnp.concatenate(rows, axis=0).T[0:64, 0:192]


def in_hbm(arrays):
    return [pltpu.with_memory_space_constraint(one, pltpu.HBM) for one in arrays]


def call(kernel, outs, in_specs, name, flops=0, moved=0, grant=32, **more):
    return pl.pallas_call(
        kernel,
        out_shape=outs,
        in_specs=in_specs,
        out_specs=more.pop("out_specs", jax.tree.map(lambda _: VMEM, outs)),
        compiler_params=pltpu.CompilerParams(vmem_limit_bytes=grant * MEBI),
        cost_estimate=pl.CostEstimate(flops=flops, bytes_accessed=moved, transcendentals=0),
        name=name,
        **more,
    )


def pairs_of(seq_count):
    return [[slot_of(m, half) * seq_count + s for m in range(2) for s in range(seq_count)] for half in range(2)]


def per_device(
    gen_features,
    gen_gain,
    gen_weight,
    flow_noise,
    time_steps,
    embed_weight,
    norm_gain,
    qkv_weight,
    qk_gain,
    out_weight,
):
    shape = jax.ShapeDtypeStruct
    seq_count = lax.axis_size("seq")
    group = lax.axis_size("mp") * lax.axis_size("dp")
    features = gen_features[0]
    tokens, width = features.shape
    local = [time_steps] + in_hbm((features, gen_gain, gen_weight.T, flow_noise[0].T))
    buffers = [
        pltpu.VMEM((tokens, width), BF16),
        pltpu.VMEM((width,), BF16),
        pltpu.VMEM((64, width), BF16),
        pltpu.VMEM((64, tokens), BF16),
    ]
    send = call(
        latents_kernel,
        shape((seq_count, 64, tokens), BF16),
        [SMEM] + [HBM] * 4,
        "latents",
        flops=2 * tokens * width * 64,
        moved=2 * tokens * width,
        scratch_shapes=buffers + [pltpu.SemaphoreType.DMA((9,))],
    )(*local)
    every_latent = lax.all_to_all(send, "seq", 0, 0)

    fold, scale = call(
        fold_kernel,
        (shape((384, 256), BF16), shape((136, 128), F32)),
        [SMEM] + [HBM] * 5,
        "fold",
        flops=2 * width * 384 * 256,
        moved=2 * width * 384,
        scratch_shapes=[
            pltpu.VMEM((64, width), BF16),
            pltpu.VMEM((2, width), BF16),
            pltpu.VMEM((3, width, 128), BF16),
            pltpu.VMEM((2, 128), BF16),
            pltpu.VMEM((64, 128), BF16),
            pltpu.SemaphoreType.DMA((7,)),
        ],
    )(
        time_steps,
        *in_hbm((embed_weight, norm_gain, qkv_weight.transpose(0, 2, 1, 3), qk_gain, out_weight.transpose(0, 2, 1))),
    )
    picked, own = call(
        own_kernel,
        (shape((width // 2, tokens), BF16), shape((72, tokens), F32)),
        [SMEM] + [HBM] * 4,
        "own",
        flops=2 * tokens * width * 64,
        moved=2 * tokens * width,
        scratch_shapes=buffers + [pltpu.VMEM((width, tokens), BF16), pltpu.SemaphoreType.DMA((4,))],
    )(*local)
    fold, scale, picked, own = lax.optimization_barrier((fold, scale, picked, own))
    keys = seq_count * tokens
    send = call(
        attention_kernel,
        shape((2 * seq_count, 32, 128), BF16),
        [VMEM] * 3,
        "attention",
        flops=2 * keys * (keys // 2) * 256,
        moved=2 * keys * 64,
        scratch_shapes=[
            pltpu.VMEM((256, keys), BF16),
            pltpu.VMEM((256, keys // 2), BF16),
        ],
    )(every_latent, fold, scale)
    whole = ("mp", "seq")
    velocities = lax.all_to_all(send, whole, 0, 0, axis_index_groups=pairs_of(seq_count))
    send, gap = call(
        gap_kernel,
        (shape((seq_count, 56, 128), BF16), shape((32, 128), F32)),
        [SMEM] + [VMEM] * 3,
        "gap",
        flops=2 * tokens * width * 16,
        moved=2 * 64 * 32 * 128,
    )(time_steps, velocities, picked, own)
    other = lax.ppermute(gap, "mp", [(slot_of(m, h), slot_of(m, 1 - h)) for m in range(2) for h in range(2)])
    partials = lax.all_to_all(send, "seq", 0, 0)
    send = call(
        total_kernel,
        shape((group, 56, 128), BF16),
        [VMEM],
        "total",
        flops=seq_count * 56 * 128,
        moved=2 * seq_count * 56 * 128,
    )(partials)
    every_total = lax.all_to_all(send, ("mp", "dp"), 0, 0)
    dmd, grad = call(
        result_kernel,
        (shape((64, tokens), F32), shape((64, width // seq_count), F32)),
        [VMEM] * 3,
        "result",
        flops=group * 24 * 128,
        moved=2 * group * 24 * 128,
    )(every_total, gap, other)
    return dmd.T[None], grad.T


def solution(mesh):
    placed = (
        P("dp", "seq", None),
        P(),
        P(),
        P("dp", "seq", None),
        P("dp"),
        P(),
        P(),
        P(None, None, None, "seq"),
        P(),
        P(),
    )
    return jax.shard_map(
        per_device,
        mesh=mesh,
        in_specs=placed,
        out_specs=(P("dp", "seq", None), P("seq", None)),
        check_vma=False,
    )
```

```python
import math

import jax
import jax.numpy as jnp
from jax import lax
from jax.experimental import pallas as pl
from jax.experimental.pallas import tpu as pltpu
from jax.sharding import PartitionSpec as P

F32 = jnp.float32
BF16 = jnp.bfloat16
STEPS = 1000
NN = (((1,), (0,)), ((), ()))
NT = (((1,), (1,)), ((), ()))
TN = (((0,), (0,)), ((), ()))
VMEM = pl.BlockSpec(memory_space=pltpu.VMEM)
SMEM = pl.BlockSpec(memory_space=pltpu.SMEM)
HBM = pl.BlockSpec(memory_space=pltpu.HBM)
MEBI = 1024 * 1024


def dot(left, right, dims=NN):
    return lax.dot_general(left, right, dims, preferred_element_type=F32)


def split_two(values):
    high = values.astype(BF16)
    low = (values - high.astype(F32)).astype(BF16)
    return high, low


def place():
    slot = lax.axis_index("mp")
    half = slot // 2
    return slot, (slot + half) % 2, half


def slot_of(model, half):
    return 2 * half + (model + half) % 2


SEQ_ORDER = list(range(15, -1, -1))
LAST_ORDER = list(range(15, -1, -1))
MODEL_ORDER = [1, 0]


def level_of(steps_ref):
    return (steps_ref[0].astype(F32) + 1.0) * (1.0 / (STEPS + 1.0))


def time_embedding(step_value, width):
    half_width = width // 2
    ranks = lax.broadcasted_iota(jnp.int32, (1, half_width), 1).astype(F32) / half_width
    phases = step_value * jnp.exp(-math.log(10000.0) * ranks)
    return jnp.concatenate([jnp.cos(phases), jnp.sin(phases)], axis=1)


def scaled_and_rms(features, gain):
    features_f = features.astype(F32)
    mean_square = jnp.sum(features_f * features_f, axis=1, keepdims=True) / features.shape[1]
    return (features_f * gain).astype(BF16), lax.rsqrt(mean_square + 1e-06)


def latents_kernel(steps_ref, features_hbm, gain_hbm, weight_hbm, noise_hbm, send_ref, features, gain, weight, noise, sems):
    _, _, half = place()
    tokens, width = features.shape
    part = tokens // 2
    copies = [
        pltpu.make_async_copy(gain_hbm, gain, sems.at[0]),
        pltpu.make_async_copy(noise_hbm, noise, sems.at[2]),
    ]
    parts = 2
    chunk = width // parts
    pieces = []
    for k in range(parts):
        span = pl.ds(k * chunk, chunk)
        group = [pltpu.make_async_copy(weight_hbm.at[:, span], weight.at[:, span], sems.at[3 + 3 * k])]
        for i in range(2):
            start = pl.multiple_of(((half + i) % 2) * part, part)
            here = features.at[pl.ds(i * part, part), span]
            group.append(pltpu.make_async_copy(features_hbm.at[pl.ds(start, part), span], here, sems.at[4 + 3 * k + i]))
        pieces.append(group)
    for copy in copies[:1] + sum(pieces, []) + copies[1:]:
        copy.start()
    level = level_of(steps_ref)
    copies[0].wait()
    gain_row = gain[...].astype(F32).reshape(1, width)
    clean = jnp.zeros((64, tokens), F32)
    squares = jnp.zeros((tokens, 128), F32)
    for k in range(parts):
        for copy in pieces[k]:
            copy.wait()
        span = slice(k * chunk, (k + 1) * chunk)
        values = features[:, span].astype(F32)
        for j in range(chunk // 128):
            one = values[:, j * 128 : (j + 1) * 128]
            squares += one * one
        clean += dot(weight[:, span], (values * gain_row[:, span]).astype(BF16), NT)
    mean_square = jnp.sum(squares, axis=1, keepdims=True) / width
    inv_row = lax.rsqrt(jnp.broadcast_to(mean_square, (tokens, tokens)).T[0:1] + 1e-06)
    clean = clean * inv_row
    copies[1].wait()
    noise_here = pltpu.roll(noise[...].astype(F32), (tokens - half * part) % tokens, 1)
    rounded = ((1.0 - level) * clean + level * noise_here).astype(BF16)
    for target in range(send_ref.shape[0]):
        send_ref[target] = rounded


def own_kernel(steps_ref, features_hbm, gain_hbm, weight_hbm, noise_hbm, picked_ref, own_ref, features, gain, weight, noise, turned, sems):
    _, model, half = place()
    width = features.shape[1]
    pairs = ((gain_hbm, gain), (features_hbm, features), (weight_hbm, weight), (noise_hbm, noise))
    copies = [pltpu.make_async_copy(source, target, sems.at[i]) for i, (source, target) in enumerate(pairs)]
    for copy in copies:
        copy.start()
    for copy in copies:
        copy.wait()
    level = level_of(steps_ref)
    scaled, inv_rms = scaled_and_rms(features[...], gain[...].astype(F32).reshape(1, width))
    inv_row = jnp.broadcast_to(inv_rms, (128, 128)).T[0:1]
    clean = dot(weight[...], scaled, NT) * inv_row
    noisy = (1.0 - level) * clean + level * noise[...].astype(F32)
    first = half == 0
    own_ref[0:32, :] = jnp.where(first, packed(clean, 0), packed(clean, 1))
    own_ref[32:64, :] = jnp.where(first, packed(noisy, 0), packed(noisy, 1))
    inverse = jnp.broadcast_to(inv_row, (8, 128))
    left = lax.broadcasted_iota(jnp.int32, (8, 128), 1) < 64
    turned_row = pltpu.roll(inverse, 64, 1)
    own_ref[64:72, :] = jnp.where(left, jnp.where(first, inverse, turned_row), jnp.where(first, turned_row, inverse))
    turned[...] = scaled.T
    for s in range(16):
        start = pl.multiple_of(SEQ_ORDER[s] * 192 + model * 96, 32)
        picked_ref[s * 96 : (s + 1) * 96, :] = turned[pl.ds(start, 96), :]


def fold_kernel(steps_ref, embed_hbm, gain_hbm, qkv_hbm, qk_hbm, out_hbm, fold_ref, scale_ref, embed, gain, qkv, qk, out, sems):
    _, model, _ = place()
    head = lax.axis_index("seq")
    width = embed.shape[1]
    parts = 3
    chunk = width // parts
    columns = pl.ds(pl.multiple_of(head * 128, 128), 128)
    pairs = ((embed_hbm.at[model], embed), (gain_hbm, gain), (qk_hbm.at[model], qk), (out_hbm.at[model, :, columns], out))
    copies = [pltpu.make_async_copy(source, target, sems.at[i]) for i, (source, target) in enumerate(pairs)]
    pieces = []
    for k in range(parts):
        span = pl.ds(k * chunk, chunk)
        pieces.append(pltpu.make_async_copy(qkv_hbm.at[model, :, span, :], qkv.at[:, span, :], sems.at[4 + k]))
    for copy in copies + pieces:
        copy.start()
    temb = time_embedding(steps_ref[0].astype(F32), width)
    squares = jnp.sum(temb * temb, axis=1, keepdims=True)
    spot = lax.broadcasted_iota(jnp.int32, (16, width), 0)
    temb_one = temb.astype(BF16).astype(F32)
    temb_two = (temb - temb_one).astype(BF16).astype(F32)
    temb_three = temb - temb_one - temb_two
    temb_rows = jnp.where(spot == 0, temb_one, jnp.where(spot == 1, temb_two, jnp.where(spot == 2, temb_three, 0.0))).astype(BF16)
    for copy in copies:
        copy.wait()
    gain_row = jnp.where(model == 0, gain[0:1, :].astype(F32), gain[1:2, :].astype(F32))
    table = embed[...]
    high, low = split_two(table.astype(F32) * gain_row)
    biased = temb * gain_row
    bias_high = biased.astype(BF16).astype(F32)
    bias_rows = jnp.where(spot == 0, bias_high, jnp.where(spot == 1, biased - bias_high, 0.0)).astype(BF16)
    rows = jnp.concatenate([high, low, bias_rows], axis=0)
    pads = jnp.zeros((48, width), BF16)
    inner = dot(table, jnp.concatenate([table, temb_rows, pads], axis=0), NT)
    acc = jnp.zeros((144, 384), F32)
    for k in range(parts):
        pieces[k].wait()
        span = slice(k * chunk, (k + 1) * chunk)
        acc += dot(rows[:, span], jnp.concatenate([qkv[i, span, :] for i in range(3)], axis=1))
    lane = lax.broadcasted_iota(jnp.int32, (64, 128), 1)
    row = lax.broadcasted_iota(jnp.int32, (64, 128), 0)

    def stacked(i):
        whole = acc[:, i * 128 : (i + 1) * 128]
        bias = whole[128:129] + whole[129:130]
        return jnp.concatenate([whole[0:64] + whole[64:128], jnp.where(row == 0, bias, 0.0)], axis=0)

    value_high, value_low = split_two(stacked(2))
    mixed = dot(out[...], value_high, NT) + dot(out[...], value_low, NT)
    linear = inner[:, 64:65] + inner[:, 65:66] + inner[:, 66:67]
    inner = jnp.where(lane < 64, inner, jnp.where(lane == 64, 2.0 * linear, 0.0))
    high, low = split_two(jnp.concatenate([stacked(1).T, mixed, inner, stacked(0).T], axis=0))
    fold_ref[...] = jnp.concatenate([high, low], axis=1)
    gains = qk[0:1, :].astype(F32) * qk[1:2, :].astype(F32) * (math.log2(math.e) / math.sqrt(128.0))
    scale_ref[0:128, :] = jnp.broadcast_to(gains, (128, 128)).T
    scale_ref[128:136, :] = jnp.broadcast_to(squares, (8, 128))


def packed(block, odd):
    left = lax.broadcasted_iota(jnp.int32, (32, 128), 1) < 64
    if odd:
        return jnp.where(left, pltpu.roll(block[0:32], 64, 1), block[32:64])
    return jnp.where(left, block[0:32], pltpu.roll(block[32:64], 64, 1))


def attention_kernel(latent_ref, fold_ref, scale_ref, send_ref, latents, queries):
    blocks = latent_ref.shape[0]
    keys = blocks * 128
    count = blocks * 64
    for table in (latents, queries):
        table[64:128, :] = jnp.ones((64, table.shape[1]), BF16)
        table[192:256, :] = jnp.ones((64, table.shape[1]), BF16)
    for s in range(blocks):
        block = latent_ref[s]
        latents[0:64, s * 128 : (s + 1) * 128] = block
        latents[128:192, s * 128 : (s + 1) * 128] = block
    for g in range(blocks // 2):
        pieces = jnp.concatenate([latent_ref[2 * g + i][:, 0:64] for i in range(2)], axis=1)
        queries[0:64, g * 128 : (g + 1) * 128] = pieces
        queries[128:192, g * 128 : (g + 1) * 128] = pieces
    squares = scale_ref[128:129, 0:1]

    def hidden_square(inner, rows):
        total = jnp.sum(inner * rows.astype(F32), axis=0, keepdims=True) + squares
        return jnp.maximum(total, 0.0) / 3072.0 + 1e-06

    projected = dot(fold_ref[0:256], latents[...])
    hidden = hidden_square(projected[192:256], latents[0:64])
    key = projected[0:128]
    key_scale = lax.rsqrt(jnp.mean(key * key, axis=0, keepdims=True) + 1e-06 * hidden)
    key = (key * key_scale).astype(BF16).T
    value = (projected[128:192] * lax.rsqrt(hidden)).astype(BF16)
    value = jnp.concatenate([value, jnp.ones((16, keys), BF16)], axis=0)
    projected = dot(fold_ref[192:384], queries[...])
    hidden = hidden_square(projected[0:64], queries[0:64])
    query = projected[64:192]
    query_scale = lax.rsqrt(jnp.mean(query * query, axis=0, keepdims=True) + 1e-06 * hidden)
    query = query * query_scale * jnp.concatenate([scale_ref[0:128]] * (count // 128), axis=1)
    query = query.astype(BF16)
    total = jnp.zeros((80, count), F32)
    step = 512
    for c in range(keys // step):
        span = slice(c * step, (c + 1) * step)
        shares = jnp.exp2(dot(key[span], query)).astype(BF16)
        total += dot(value[:, span], shares)
    mixed = total[0:64] / total[64:65]
    for s in range(blocks):
        block = packed(mixed[:, (s // 2) * 128 : (s // 2 + 1) * 128], s % 2).astype(BF16)
        send_ref[s] = block
        send_ref[blocks + s] = block


def gap_kernel(steps_ref, velocity_ref, picked_ref, own_ref, send_ref, gap_ref):
    level = level_of(steps_ref)
    _, _, half = place()
    sums = [jnp.sum(velocity_ref[16 * i : 16 * i + 16].astype(F32), axis=0) for i in range(2)]
    teacher = sums[MODEL_ORDER.index(0)]
    gap = level * (teacher - sums[MODEL_ORDER.index(1)])
    gap_ref[...] = gap
    distance = jnp.abs(own_ref[0:32] - (own_ref[32:64] - level * teacher))
    spread = jnp.sum(jnp.sum(distance, axis=1, keepdims=True), axis=0, keepdims=True)
    direction = gap * own_ref[64:65]
    turned = pltpu.roll(direction, 64, 1)
    left = lax.broadcasted_iota(jnp.int32, (64, 128), 1) < 64
    rows = jnp.where(
        half == 0,
        jnp.where(left, jnp.concatenate([direction, turned], axis=0), 0.0),
        jnp.where(left, 0.0, jnp.concatenate([turned, direction], axis=0)),
    ).astype(BF16)
    grad = dot(picked_ref[...], jnp.concatenate([rows, rows], axis=0), NT)
    tail = spread_rows(spread)
    left = left[0:48]
    for s in range(send_ref.shape[0]):
        pair = jnp.where(left, grad[s * 96 : s * 96 + 48], grad[s * 96 + 48 : s * 96 + 96])
        send_ref[s] = jnp.concatenate([pair, tail], axis=0).astype(BF16)


def spread_rows(spread):
    spread = jnp.broadcast_to(spread, (8, 128))
    spot = lax.broadcasted_iota(jnp.int32, (8, 128), 0)
    high = spread.astype(BF16).astype(F32)
    return jnp.where(spot == 0, high, jnp.where(spot == 1, spread - high, 0.0))


def total_kernel(grad_ref, send_ref):
    total = jnp.sum(grad_ref[...].astype(F32), axis=0)
    tail = spread_rows(total[48:49] + total[49:50])
    whole = jnp.concatenate([total[0:48], tail], axis=0).astype(BF16)
    for target in range(send_ref.shape[0]):
        send_ref[target] = whole


def result_kernel(all_ref, gap_ref, other_ref, dmd_ref, grad_ref):
    _, _, half = place()
    sample = lax.axis_index("dp")
    totals = [jnp.zeros((48, 128), F32)] * 2
    mine = jnp.zeros((1, 128), F32)
    for d in range(4):
        sums = [sum(all_ref[LAST_ORDER.index(slot_of(m, h) + 4 * d)].astype(F32) for h in range(2)) for m in range(2)]
        inverse = 1.0 / ((sums[0][48:49] + sums[0][49:50]) / 131072.0 + 1e-05)
        mine = jnp.where(sample == d, inverse, mine)
        totals = [total + one[0:48] * inverse for total, one in zip(totals, sums)]
    own = gap_ref[...] * mine
    other = other_ref[...] * mine
    first = jnp.where(half == 0, own, other)
    second = jnp.where(half == 0, other, own)
    left = lax.broadcasted_iota(jnp.int32, (32, 128), 1) < 64
    dmd_ref[0:32, :] = jnp.where(left, first, pltpu.roll(second, 64, 1))
    dmd_ref[32:64, :] = jnp.where(left, pltpu.roll(first, 64, 1), second)
    rows = []
    for total in totals:
        rows += [total, pltpu.roll(total, 64, 1)]
    rows.append(jnp.zeros((64, 128), F32))
    grad_ref[...] = jnp.concatenate(rows, axis=0).T[0:64, 0:192]


def in_hbm(arrays):
    return [pltpu.with_memory_space_constraint(one, pltpu.HBM) for one in arrays]


def call(kernel, outs, in_specs, name, flops=0, moved=0, grant=32, **more):
    return pl.pallas_call(
        kernel,
        out_shape=outs,
        in_specs=in_specs,
        out_specs=more.pop("out_specs", jax.tree.map(lambda _: VMEM, outs)),
        compiler_params=pltpu.CompilerParams(vmem_limit_bytes=grant * MEBI),
        cost_estimate=pl.CostEstimate(flops=flops, bytes_accessed=moved, transcendentals=0),
        name=name,
        **more,
    )


def pairs_of(seq_count):
    return [[slot_of(m, half) * seq_count + s for m in MODEL_ORDER for s in SEQ_ORDER] for half in range(2)]


def per_device(
    gen_features,
    gen_gain,
    gen_weight,
    flow_noise,
    time_steps,
    embed_weight,
    norm_gain,
    qkv_weight,
    qk_gain,
    out_weight,
):
    shape = jax.ShapeDtypeStruct
    seq_count = lax.axis_size("seq")
    group = lax.axis_size("mp") * lax.axis_size("dp")
    features = gen_features[0]
    tokens, width = features.shape
    local = [time_steps] + in_hbm((features, gen_gain, gen_weight.T, flow_noise[0].T))
    buffers = [
        pltpu.VMEM((tokens, width), BF16),
        pltpu.VMEM((width,), BF16),
        pltpu.VMEM((64, width), BF16),
        pltpu.VMEM((64, tokens), BF16),
    ]
    send = call(
        latents_kernel,
        shape((seq_count, 64, tokens), BF16),
        [SMEM] + [HBM] * 4,
        "latents",
        flops=2 * tokens * width * 64,
        moved=2 * tokens * width,
        scratch_shapes=buffers + [pltpu.SemaphoreType.DMA((9,))],
    )(*local)
    every_latent = lax.all_to_all(send, "seq", 0, 0, axis_index_groups=[SEQ_ORDER])

    fold, scale = call(
        fold_kernel,
        (shape((384, 256), BF16), shape((136, 128), F32)),
        [SMEM] + [HBM] * 5,
        "fold",
        flops=2 * width * 384 * 256,
        moved=2 * width * 384,
        scratch_shapes=[
            pltpu.VMEM((64, width), BF16),
            pltpu.VMEM((2, width), BF16),
            pltpu.VMEM((3, width, 128), BF16),
            pltpu.VMEM((2, 128), BF16),
            pltpu.VMEM((64, 128), BF16),
            pltpu.SemaphoreType.DMA((7,)),
        ],
    )(
        time_steps,
        *in_hbm((embed_weight, norm_gain, qkv_weight.transpose(0, 2, 1, 3), qk_gain, out_weight.transpose(0, 2, 1))),
    )
    picked, own = call(
        own_kernel,
        (shape((width // 2, tokens), BF16), shape((72, tokens), F32)),
        [SMEM] + [HBM] * 4,
        "own",
        flops=2 * tokens * width * 64,
        moved=2 * tokens * width,
        scratch_shapes=buffers + [pltpu.VMEM((width, tokens), BF16), pltpu.SemaphoreType.DMA((4,))],
    )(*local)
    fold, scale, picked, own = lax.optimization_barrier((fold, scale, picked, own))
    keys = seq_count * tokens
    send = call(
        attention_kernel,
        shape((2 * seq_count, 32, 128), BF16),
        [VMEM] * 3,
        "attention",
        flops=2 * keys * (keys // 2) * 256,
        moved=2 * keys * 64,
        scratch_shapes=[
            pltpu.VMEM((256, keys), BF16),
            pltpu.VMEM((256, keys // 2), BF16),
        ],
    )(every_latent, fold, scale)
    whole = ("mp", "seq")
    velocities = lax.all_to_all(send, whole, 0, 0, axis_index_groups=pairs_of(seq_count))
    send, gap = call(
        gap_kernel,
        (shape((seq_count, 56, 128), BF16), shape((32, 128), F32)),
        [SMEM] + [VMEM] * 3,
        "gap",
        flops=2 * tokens * width * 16,
        moved=2 * 64 * 32 * 128,
    )(time_steps, velocities, picked, own)
    other = lax.ppermute(gap, "mp", [(slot_of(m, h), slot_of(m, 1 - h)) for m in range(2) for h in range(2)])
    partials = lax.all_to_all(send, "seq", 0, 0, axis_index_groups=[SEQ_ORDER])
    send = call(
        total_kernel,
        shape((group, 56, 128), BF16),
        [VMEM],
        "total",
        flops=seq_count * 56 * 128,
        moved=2 * seq_count * 56 * 128,
    )(partials)
    every_total = lax.all_to_all(send, ("dp", "mp"), 0, 0, axis_index_groups=[LAST_ORDER])
    dmd, grad = call(
        result_kernel,
        (shape((64, tokens), F32), shape((64, width // seq_count), F32)),
        [VMEM] * 3,
        "result",
        flops=group * 24 * 128,
        moved=2 * group * 24 * 128,
    )(every_total, gap, other)
    return dmd.T[None], grad.T


def solution(mesh):
    placed = (
        P("dp", "seq", None),
        P(),
        P(),
        P("dp", "seq", None),
        P("dp"),
        P(),
        P(),
        P(None, None, None, "seq"),
        P(),
        P(),
    )
    return jax.shard_map(
        per_device,
        mesh=mesh,
        in_specs=placed,
        out_specs=(P("dp", "seq", None), P("seq", None)),
        check_vma=False,
    )
```

```python
import math

import jax
import jax.numpy as jnp
from jax import lax
from jax.experimental import pallas as pl
from jax.experimental.pallas import tpu as pltpu
from jax.sharding import PartitionSpec as P

F32 = jnp.float32
BF16 = jnp.bfloat16
STEPS = 1000
NN = (((1,), (0,)), ((), ()))
NT = (((1,), (1,)), ((), ()))
TN = (((0,), (0,)), ((), ()))
VMEM = pl.BlockSpec(memory_space=pltpu.VMEM)
SMEM = pl.BlockSpec(memory_space=pltpu.SMEM)
HBM = pl.BlockSpec(memory_space=pltpu.HBM)
MEBI = 1024 * 1024


def dot(left, right, dims=NN):
    return lax.dot_general(left, right, dims, preferred_element_type=F32)


def split_two(values):
    high = values.astype(BF16)
    low = (values - high.astype(F32)).astype(BF16)
    return high, low


def place():
    slot = lax.axis_index("mp")
    half = slot // 2
    return slot, (slot + half) % 2, half


def slot_of(model, half):
    return 2 * half + (model + half) % 2


SEQ_ORDER = list(range(15, -1, -1))
LAST_ORDER = [4 * d + m for d in (2, 3, 0, 1) for m in (3, 2, 1, 0)]
MODEL_ORDER = [1, 0]


def level_of(steps_ref):
    return (steps_ref[0].astype(F32) + 1.0) * (1.0 / (STEPS + 1.0))


def time_embedding(step_value, width):
    half_width = width // 2
    ranks = lax.broadcasted_iota(jnp.int32, (1, half_width), 1).astype(F32) / half_width
    phases = step_value * jnp.exp(-math.log(10000.0) * ranks)
    return jnp.concatenate([jnp.cos(phases), jnp.sin(phases)], axis=1)


def scaled_and_rms(features, gain):
    features_f = features.astype(F32)
    mean_square = jnp.sum(features_f * features_f, axis=1, keepdims=True) / features.shape[1]
    return (features_f * gain).astype(BF16), lax.rsqrt(mean_square + 1e-06)


def latents_kernel(steps_ref, features_hbm, gain_hbm, weight_hbm, noise_hbm, send_ref, features, gain, weight, noise, sems):
    _, _, half = place()
    tokens, width = features.shape
    part = tokens // 2
    copies = [
        pltpu.make_async_copy(gain_hbm, gain, sems.at[0]),
        pltpu.make_async_copy(noise_hbm, noise, sems.at[2]),
    ]
    parts = 2
    chunk = width // parts
    pieces = []
    for k in range(parts):
        span = pl.ds(k * chunk, chunk)
        group = [pltpu.make_async_copy(weight_hbm.at[:, span], weight.at[:, span], sems.at[3 + 3 * k])]
        for i in range(2):
            start = pl.multiple_of(((half + i) % 2) * part, part)
            here = features.at[pl.ds(i * part, part), span]
            group.append(pltpu.make_async_copy(features_hbm.at[pl.ds(start, part), span], here, sems.at[4 + 3 * k + i]))
        pieces.append(group)
    for copy in copies[:1] + sum(pieces, []) + copies[1:]:
        copy.start()
    level = level_of(steps_ref)
    copies[0].wait()
    gain_row = gain[...].astype(F32).reshape(1, width)
    clean = jnp.zeros((64, tokens), F32)
    squares = jnp.zeros((tokens, 128), F32)
    for k in range(parts):
        for copy in pieces[k]:
            copy.wait()
        span = slice(k * chunk, (k + 1) * chunk)
        values = features[:, span].astype(F32)
        for j in range(chunk // 128):
            one = values[:, j * 128 : (j + 1) * 128]
            squares += one * one
        clean += dot(weight[:, span], (values * gain_row[:, span]).astype(BF16), NT)
    mean_square = jnp.sum(squares, axis=1, keepdims=True) / width
    inv_row = lax.rsqrt(jnp.broadcast_to(mean_square, (tokens, tokens)).T[0:1] + 1e-06)
    clean = clean * inv_row
    copies[1].wait()
    noise_here = pltpu.roll(noise[...].astype(F32), (tokens - half * part) % tokens, 1)
    rounded = ((1.0 - level) * clean + level * noise_here).astype(BF16)
    for target in range(send_ref.shape[0]):
        send_ref[target] = rounded


def own_kernel(steps_ref, features_hbm, gain_hbm, weight_hbm, noise_hbm, picked_ref, own_ref, features, gain, weight, noise, turned, sems):
    _, model, half = place()
    width = features.shape[1]
    pairs = ((gain_hbm, gain), (features_hbm, features), (weight_hbm, weight), (noise_hbm, noise))
    copies = [pltpu.make_async_copy(source, target, sems.at[i]) for i, (source, target) in enumerate(pairs)]
    for copy in copies:
        copy.start()
    for copy in copies:
        copy.wait()
    level = level_of(steps_ref)
    scaled, inv_rms = scaled_and_rms(features[...], gain[...].astype(F32).reshape(1, width))
    inv_row = jnp.broadcast_to(inv_rms, (128, 128)).T[0:1]
    clean = dot(weight[...], scaled, NT) * inv_row
    noisy = (1.0 - level) * clean + level * noise[...].astype(F32)
    first = half == 0
    own_ref[0:32, :] = jnp.where(first, packed(clean, 0), packed(clean, 1))
    own_ref[32:64, :] = jnp.where(first, packed(noisy, 0), packed(noisy, 1))
    inverse = jnp.broadcast_to(inv_row, (8, 128))
    left = lax.broadcasted_iota(jnp.int32, (8, 128), 1) < 64
    turned_row = pltpu.roll(inverse, 64, 1)
    own_ref[64:72, :] = jnp.where(left, jnp.where(first, inverse, turned_row), jnp.where(first, turned_row, inverse))
    turned[...] = scaled.T
    for s in range(16):
        start = pl.multiple_of(SEQ_ORDER[s] * 192 + model * 96, 32)
        picked_ref[s * 96 : (s + 1) * 96, :] = turned[pl.ds(start, 96), :]


def fold_kernel(steps_ref, embed_hbm, gain_hbm, qkv_hbm, qk_hbm, out_hbm, fold_ref, scale_ref, embed, gain, qkv, qk, out, sems):
    _, model, _ = place()
    head = lax.axis_index("seq")
    width = embed.shape[1]
    parts = 3
    chunk = width // parts
    columns = pl.ds(pl.multiple_of(head * 128, 128), 128)
    pairs = ((embed_hbm.at[model], embed), (gain_hbm, gain), (qk_hbm.at[model], qk), (out_hbm.at[model, :, columns], out))
    copies = [pltpu.make_async_copy(source, target, sems.at[i]) for i, (source, target) in enumerate(pairs)]
    pieces = []
    for k in range(parts):
        span = pl.ds(k * chunk, chunk)
        pieces.append(pltpu.make_async_copy(qkv_hbm.at[model, :, span, :], qkv.at[:, span, :], sems.at[4 + k]))
    for copy in copies + pieces:
        copy.start()
    temb = time_embedding(steps_ref[0].astype(F32), width)
    squares = jnp.sum(temb * temb, axis=1, keepdims=True)
    spot = lax.broadcasted_iota(jnp.int32, (16, width), 0)
    temb_one = temb.astype(BF16).astype(F32)
    temb_two = (temb - temb_one).astype(BF16).astype(F32)
    temb_three = temb - temb_one - temb_two
    temb_rows = jnp.where(spot == 0, temb_one, jnp.where(spot == 1, temb_two, jnp.where(spot == 2, temb_three, 0.0))).astype(BF16)
    for copy in copies:
        copy.wait()
    gain_row = jnp.where(model == 0, gain[0:1, :].astype(F32), gain[1:2, :].astype(F32))
    table = embed[...]
    high, low = split_two(table.astype(F32) * gain_row)
    biased = temb * gain_row
    bias_high = biased.astype(BF16).astype(F32)
    bias_rows = jnp.where(spot == 0, bias_high, jnp.where(spot == 1, biased - bias_high, 0.0)).astype(BF16)
    rows = jnp.concatenate([high, low, bias_rows], axis=0)
    pads = jnp.zeros((48, width), BF16)
    inner = dot(table, jnp.concatenate([table, temb_rows, pads], axis=0), NT)
    acc = jnp.zeros((144, 384), F32)
    for k in range(parts):
        pieces[k].wait()
        span = slice(k * chunk, (k + 1) * chunk)
        acc += dot(rows[:, span], jnp.concatenate([qkv[i, span, :] for i in range(3)], axis=1))
    lane = lax.broadcasted_iota(jnp.int32, (64, 128), 1)
    row = lax.broadcasted_iota(jnp.int32, (64, 128), 0)

    def stacked(i):
        whole = acc[:, i * 128 : (i + 1) * 128]
        bias = whole[128:129] + whole[129:130]
        return jnp.concatenate([whole[0:64] + whole[64:128], jnp.where(row == 0, bias, 0.0)], axis=0)

    value_high, value_low = split_two(stacked(2))
    mixed = dot(out[...], value_high, NT) + dot(out[...], value_low, NT)
    linear = inner[:, 64:65] + inner[:, 65:66] + inner[:, 66:67]
    inner = jnp.where(lane < 64, inner, jnp.where(lane == 64, 2.0 * linear, 0.0))
    high, low = split_two(jnp.concatenate([stacked(1).T, mixed, inner, inner, stacked(0).T], axis=0))
    whole = jnp.concatenate([high, low], axis=1)
    rest = (inner - high[192:256].astype(F32) - low[192:256].astype(F32)).astype(BF16)
    fold_ref[0:192, :] = whole[0:192]
    fold_ref[192:256, :] = jnp.concatenate([rest, jnp.zeros((64, 128), BF16)], axis=1)
    fold_ref[256:448, :] = whole[256:448]
    gains = qk[0:1, :].astype(F32) * qk[1:2, :].astype(F32) * (math.log2(math.e) / math.sqrt(128.0))
    scale_ref[0:128, :] = jnp.broadcast_to(gains, (128, 128)).T
    scale_ref[128:136, :] = jnp.broadcast_to(squares, (8, 128))


def packed(block, odd):
    left = lax.broadcasted_iota(jnp.int32, (32, 128), 1) < 64
    if odd:
        return jnp.where(left, pltpu.roll(block[0:32], 64, 1), block[32:64])
    return jnp.where(left, block[0:32], pltpu.roll(block[32:64], 64, 1))


def attention_kernel(latent_ref, fold_ref, scale_ref, send_ref, latents, queries):
    blocks = latent_ref.shape[0]
    keys = blocks * 128
    count = blocks * 64
    for table in (latents, queries):
        table[64:128, :] = jnp.ones((64, table.shape[1]), BF16)
        table[192:256, :] = jnp.ones((64, table.shape[1]), BF16)
    for s in range(blocks):
        block = latent_ref[s]
        latents[0:64, s * 128 : (s + 1) * 128] = block
        latents[128:192, s * 128 : (s + 1) * 128] = block
    for g in range(blocks // 2):
        pieces = jnp.concatenate([latent_ref[2 * g + i][:, 0:64] for i in range(2)], axis=1)
        queries[0:64, g * 128 : (g + 1) * 128] = pieces
        queries[128:192, g * 128 : (g + 1) * 128] = pieces
    squares = scale_ref[128:129, 0:1]

    def hidden_square(inner, rows):
        total = jnp.sum(inner * rows.astype(F32), axis=0, keepdims=True) + squares
        return jnp.maximum(total, 0.0) / 3072.0 + 1e-06

    projected = dot(fold_ref[0:320], latents[...])
    hidden = hidden_square(projected[192:256] + projected[256:320], latents[0:64])
    key = projected[0:128]
    key_scale = lax.rsqrt(jnp.mean(key * key, axis=0, keepdims=True) + 1e-06 * hidden)
    key = (key * key_scale).astype(BF16).T
    value = (projected[128:192] * lax.rsqrt(hidden)).astype(BF16)
    value = jnp.concatenate([value, jnp.ones((16, keys), BF16)], axis=0)
    projected = dot(fold_ref[256:448], queries[...])
    hidden = hidden_square(projected[0:64], queries[0:64])
    query = projected[64:192]
    query_scale = lax.rsqrt(jnp.mean(query * query, axis=0, keepdims=True) + 1e-06 * hidden)
    query = query * query_scale * jnp.concatenate([scale_ref[0:128]] * (count // 128), axis=1)
    query = query.astype(BF16)
    total = jnp.zeros((80, count), F32)
    step = 512
    for c in range(keys // step):
        span = slice(c * step, (c + 1) * step)
        shares = jnp.exp2(dot(key[span], query)).astype(BF16)
        total += dot(value[:, span], shares)
    mixed = total[0:64] / total[64:65]
    for s in range(blocks):
        block = packed(mixed[:, (s // 2) * 128 : (s // 2 + 1) * 128], s % 2).astype(BF16)
        send_ref[s] = block
        send_ref[blocks + s] = block


def gap_kernel(steps_ref, velocity_ref, picked_ref, own_ref, send_ref, gap_ref):
    level = level_of(steps_ref)
    _, _, half = place()
    sums = [jnp.sum(velocity_ref[16 * i : 16 * i + 16].astype(F32), axis=0) for i in range(2)]
    teacher = sums[MODEL_ORDER.index(0)]
    gap = level * (teacher - sums[MODEL_ORDER.index(1)])
    gap_ref[...] = gap
    distance = jnp.abs(own_ref[0:32] - (own_ref[32:64] - level * teacher))
    spread = jnp.sum(jnp.sum(distance, axis=1, keepdims=True), axis=0, keepdims=True)
    direction = gap * own_ref[64:65]
    turned = pltpu.roll(direction, 64, 1)
    left = lax.broadcasted_iota(jnp.int32, (64, 128), 1) < 64
    rows = jnp.where(
        half == 0,
        jnp.where(left, jnp.concatenate([direction, turned], axis=0), 0.0),
        jnp.where(left, 0.0, jnp.concatenate([turned, direction], axis=0)),
    ).astype(BF16)
    grad = dot(picked_ref[...], jnp.concatenate([rows, rows], axis=0), NT)
    tail = spread_rows(spread)
    left = left[0:48]
    for s in range(send_ref.shape[0]):
        pair = jnp.where(left, grad[s * 96 : s * 96 + 48], grad[s * 96 + 48 : s * 96 + 96])
        send_ref[s] = jnp.concatenate([pair, tail], axis=0).astype(BF16)


def spread_rows(spread):
    spread = jnp.broadcast_to(spread, (8, 128))
    spot = lax.broadcasted_iota(jnp.int32, (8, 128), 0)
    high = spread.astype(BF16).astype(F32)
    return jnp.where(spot == 0, high, jnp.where(spot == 1, spread - high, 0.0))


def total_kernel(grad_ref, send_ref):
    total = jnp.sum(grad_ref[...].astype(F32), axis=0)
    tail = spread_rows(total[48:49] + total[49:50])
    whole = jnp.concatenate([total[0:48], tail], axis=0).astype(BF16)
    for target in range(send_ref.shape[0]):
        send_ref[target] = whole


def result_kernel(all_ref, gap_ref, other_ref, dmd_ref, grad_ref):
    _, _, half = place()
    sample = lax.axis_index("dp")
    totals = [jnp.zeros((48, 128), F32)] * 2
    mine = jnp.zeros((1, 128), F32)
    for d in range(4):
        sums = [sum(all_ref[LAST_ORDER.index(slot_of(m, h) + 4 * d)].astype(F32) for h in range(2)) for m in range(2)]
        inverse = 1.0 / ((sums[0][48:49] + sums[0][49:50]) / 131072.0 + 1e-05)
        mine = jnp.where(sample == d, inverse, mine)
        totals = [total + one[0:48] * inverse for total, one in zip(totals, sums)]
    own = gap_ref[...] * mine
    other = other_ref[...] * mine
    first = jnp.where(half == 0, own, other)
    second = jnp.where(half == 0, other, own)
    left = lax.broadcasted_iota(jnp.int32, (32, 128), 1) < 64
    dmd_ref[0:32, :] = jnp.where(left, first, pltpu.roll(second, 64, 1))
    dmd_ref[32:64, :] = jnp.where(left, pltpu.roll(first, 64, 1), second)
    rows = []
    for total in totals:
        rows += [total, pltpu.roll(total, 64, 1)]
    rows.append(jnp.zeros((64, 128), F32))
    grad_ref[...] = jnp.concatenate(rows, axis=0).T[0:64, 0:192]


def in_hbm(arrays):
    return [pltpu.with_memory_space_constraint(one, pltpu.HBM) for one in arrays]


def call(kernel, outs, in_specs, name, flops=0, moved=0, grant=32, **more):
    return pl.pallas_call(
        kernel,
        out_shape=outs,
        in_specs=in_specs,
        out_specs=more.pop("out_specs", jax.tree.map(lambda _: VMEM, outs)),
        compiler_params=pltpu.CompilerParams(vmem_limit_bytes=grant * MEBI),
        cost_estimate=pl.CostEstimate(flops=flops, bytes_accessed=moved, transcendentals=0),
        name=name,
        **more,
    )


def pairs_of(seq_count):
    return [[slot_of(m, half) * seq_count + s for m in MODEL_ORDER for s in SEQ_ORDER] for half in range(2)]


def per_device(
    gen_features,
    gen_gain,
    gen_weight,
    flow_noise,
    time_steps,
    embed_weight,
    norm_gain,
    qkv_weight,
    qk_gain,
    out_weight,
):
    shape = jax.ShapeDtypeStruct
    seq_count = lax.axis_size("seq")
    group = lax.axis_size("mp") * lax.axis_size("dp")
    features = gen_features[0]
    tokens, width = features.shape
    local = [time_steps] + in_hbm((features, gen_gain, gen_weight.T, flow_noise[0].T))
    buffers = [
        pltpu.VMEM((tokens, width), BF16),
        pltpu.VMEM((width,), BF16),
        pltpu.VMEM((64, width), BF16),
        pltpu.VMEM((64, tokens), BF16),
    ]
    send = call(
        latents_kernel,
        shape((seq_count, 64, tokens), BF16),
        [SMEM] + [HBM] * 4,
        "latents",
        flops=2 * tokens * width * 64,
        moved=2 * tokens * width,
        scratch_shapes=buffers + [pltpu.SemaphoreType.DMA((9,))],
    )(*local)
    every_latent = lax.all_to_all(send, "seq", 0, 0, axis_index_groups=[SEQ_ORDER])

    fold, scale = call(
        fold_kernel,
        (shape((448, 256), BF16), shape((136, 128), F32)),
        [SMEM] + [HBM] * 5,
        "fold",
        flops=2 * width * 384 * 256,
        moved=2 * width * 384,
        scratch_shapes=[
            pltpu.VMEM((64, width), BF16),
            pltpu.VMEM((2, width), BF16),
            pltpu.VMEM((3, width, 128), BF16),
            pltpu.VMEM((2, 128), BF16),
            pltpu.VMEM((64, 128), BF16),
            pltpu.SemaphoreType.DMA((7,)),
        ],
    )(
        time_steps,
        *in_hbm((embed_weight, norm_gain, qkv_weight.transpose(0, 2, 1, 3), qk_gain, out_weight.transpose(0, 2, 1))),
    )
    picked, own = call(
        own_kernel,
        (shape((width // 2, tokens), BF16), shape((72, tokens), F32)),
        [SMEM] + [HBM] * 4,
        "own",
        flops=2 * tokens * width * 64,
        moved=2 * tokens * width,
        scratch_shapes=buffers + [pltpu.VMEM((width, tokens), BF16), pltpu.SemaphoreType.DMA((4,))],
    )(*local)
    fold, scale, picked, own = lax.optimization_barrier((fold, scale, picked, own))
    keys = seq_count * tokens
    send = call(
        attention_kernel,
        shape((2 * seq_count, 32, 128), BF16),
        [VMEM] * 3,
        "attention",
        flops=2 * keys * (keys // 2) * 256,
        moved=2 * keys * 64,
        scratch_shapes=[
            pltpu.VMEM((256, keys), BF16),
            pltpu.VMEM((256, keys // 2), BF16),
        ],
    )(every_latent, fold, scale)
    whole = ("mp", "seq")
    velocities = lax.all_to_all(send, whole, 0, 0, axis_index_groups=pairs_of(seq_count))
    send, gap = call(
        gap_kernel,
        (shape((seq_count, 56, 128), BF16), shape((32, 128), F32)),
        [SMEM] + [VMEM] * 3,
        "gap",
        flops=2 * tokens * width * 16,
        moved=2 * 64 * 32 * 128,
    )(time_steps, velocities, picked, own)
    other = lax.ppermute(gap, "mp", [(slot_of(m, h), slot_of(m, 1 - h)) for m in range(2) for h in range(2)])
    partials = lax.all_to_all(send, "seq", 0, 0, axis_index_groups=[SEQ_ORDER])
    send = call(
        total_kernel,
        shape((group, 56, 128), BF16),
        [VMEM],
        "total",
        flops=seq_count * 56 * 128,
        moved=2 * seq_count * 56 * 128,
    )(partials)
    every_total = lax.all_to_all(send, ("dp", "mp"), 0, 0, axis_index_groups=[LAST_ORDER])
    dmd, grad = call(
        result_kernel,
        (shape((64, tokens), F32), shape((64, width // seq_count), F32)),
        [VMEM] * 3,
        "result",
        flops=group * 24 * 128,
        moved=2 * group * 24 * 128,
    )(every_total, gap, other)
    return dmd.T[None], grad.T


def solution(mesh):
    placed = (
        P("dp", "seq", None),
        P(),
        P(),
        P("dp", "seq", None),
        P("dp"),
        P(),
        P(),
        P(None, None, None, "seq"),
        P(),
        P(),
    )
    return jax.shard_map(
        per_device,
        mesh=mesh,
        in_specs=placed,
        out_specs=(P("dp", "seq", None), P("seq", None)),
        check_vma=False,
    )
```
